128 devices in a mesh: row: 8 (over y, x_lo), col: 16 (over z, x_hi, core).
Axes of the slice: x: 4 (x_hi: 2, x_lo: 2; x = x_hi * 2 + x_lo), y: 4, z: 4, core: 2. Of those that a mesh axis runs over, the one named last changes fastest.
Arguments:
- a_blocks: bfloat16 [16, 256, 128, 128], P('col', 'row'), may hold values from -0.5 to 0.5
- a_rows: int32 [16, 256], P('col', 'row'), may hold values from 0 to 7, as said below
- b_blocks: bfloat16 [8, 256, 128, 128], P('row', 'col'), may hold values from -6 to 6
- b_cols: int32 [8, 256], P('row', 'col'), may hold values from 0 to 15, as said below
- c_keep: int32 [8, 16, 96], P('row', 'col'), may hold values from 0 to 127, as said below
- c_owner: int32 [8, 16, 96], P('row', 'col'), may hold values from 0 to 127, as said below
- c_slot: int32 [8, 16, 96], P('row', 'col'), may hold values from 0 to 255, as said below
Outputs:
- owned_blocks: bfloat16 [8, 4096, 128, 128], P('row', 'col')
The draws below stay inside these ranges and needn't reach their ends.
Inputs may be any that keep to these rules, and one draw needn't show every extreme that they name: `a_rows`: for each j, i and block column c of the panel, the slots c * (2) to (c + 1) * 2 - 1 name 2 distinct rows. `b_cols`: for each i, j and block row of the half panel, its 2 consecutive slots name distinct columns. `c_keep`: the 96 positions of one device are distinct. `c_owner`: each device sends to exactly 48 distinct owners, exactly 2 blocks to each; some owner receives 256 blocks in all, none more. `c_slot`: the pairs (owner, slot) are distinct over all kept blocks of all devices.
All inputs are finite; a program needn't handle non-finite values.
Results may differ from the reference program's by a relative error of at most 0.001.
Values may be sent and summed in bfloat16 or wider, within the bound.
A program may use at most 128 MiB of HBM per device.

```python
import jax
import jax.numpy as jnp
import numpy as np
from jax import lax

BS = 128
RB = 8
CB = 16
SA = 32
SBH = 16
FANOUT = 48
KC = 96
RCAP = 256
N_ROW = 8
N_COL = 16
DEVICES = 128


def owner_plan(key):
    counts = np.concatenate([np.full(DEVICES // 8, DEVICES), np.full(DEVICES // 8, DEVICES // 2), np.full(3 * DEVICES // 4, DEVICES // 4)])
    rank_of = np.repeat(np.arange(DEVICES), counts)
    starts = np.concatenate([np.zeros(1, np.int64), np.cumsum(counts)[:-1]])
    positions = np.arange(DEVICES * FANOUT)
    offsets = positions - starts[rank_of]
    key_owner, key_source, key_slot, key_shuffle = jax.random.split(key, 4)
    owner_label = jax.random.permutation(key_owner, DEVICES).astype(jnp.int32)
    source_label = jax.random.permutation(key_source, DEVICES).astype(jnp.int32)

    def slot_order(subkey):
        return jax.random.permutation(subkey, RCAP).astype(jnp.int32)

    def kept_order(subkey):
        return jax.random.permutation(subkey, KC).astype(jnp.int32)
    slot_table = jax.vmap(slot_order)(jax.random.split(key_slot, DEVICES))
    owners = owner_label[rank_of]
    sources = source_label[positions % DEVICES]
    rounds = positions // DEVICES
    owner_grid = jnp.zeros((DEVICES, KC), jnp.int32)
    slot_grid = jnp.zeros((DEVICES, KC), jnp.int32)
    for member in range(2):
        owner_grid = owner_grid.at[sources, 2 * rounds + member].set(owners)
        slot_grid = slot_grid.at[sources, 2 * rounds + member].set(slot_table[owners, 2 * offsets + member])
    shuffle = jax.vmap(kept_order)(jax.random.split(key_shuffle, DEVICES))
    owner_grid = jnp.take_along_axis(owner_grid, shuffle, axis=1)
    slot_grid = jnp.take_along_axis(slot_grid, shuffle, axis=1)
    return (owner_grid.reshape(N_ROW, N_COL, KC), slot_grid.reshape(N_ROW, N_COL, KC))


def draw_a_rows(key, part):
    key = jax.random.fold_in(key, 11)

    def pick_rows(subkey):
        return jax.random.permutation(subkey, RB)[:RB // 4].astype(jnp.int32)
    chosen = jax.vmap(pick_rows)(jax.random.split(key, N_COL * N_ROW * CB))
    return chosen.reshape(N_COL, N_ROW * SA)


def draw_b_cols(key, part):
    key = jax.random.fold_in(key, 13)

    def pick_cols(subkey):
        return jax.random.permutation(subkey, CB)[:CB // 8].astype(jnp.int32)
    chosen = jax.vmap(pick_cols)(jax.random.split(key, N_ROW * N_COL * (CB // 2)))
    return chosen.reshape(N_ROW, N_COL * SBH)


def draw_c_keep(key, part):
    key = jax.random.fold_in(key, 17)

    def pick_kept(subkey):
        return jax.random.permutation(subkey, RB * CB)[:KC].astype(jnp.int32)
    chosen = jax.vmap(pick_kept)(jax.random.split(key, DEVICES))
    return chosen.reshape(N_ROW, N_COL, KC)


def draw_c_owner(key, part):
    plan = owner_plan(key)
    return plan[0]


def draw_c_slot(key, part):
    plan = owner_plan(key)
    return plan[1]


def shard_levels(rng, extent, pieces, smallest, top_value):
    gain = 1.0
    for dim, blocks in pieces:
        draws = jax.random.uniform(jax.random.fold_in(jax.random.fold_in(rng, 6), dim), (blocks,), jnp.float32, smallest / len(pieces), top_value / len(pieces))
        gain = gain * jnp.repeat(jnp.exp(draws), extent[dim] // blocks).reshape((-1,) + (1,) * (len(extent) - 1 - dim))
    return gain


def bell_draw(key, shape, scale, most, pieces=(), kind=jnp.bfloat16):
    level = shard_levels(key, shape, pieces, -0.22, 0.18) if pieces else 1.0
    result = jax.random.normal(key, shape, jnp.float32) * scale * level
    return jnp.minimum(jnp.maximum(result, -most), most).astype(kind)


def setup_inputs(seed: int = 0) -> dict:
    key_of = jax.random.split(jax.random.key(seed), 8)
    a_blocks = bell_draw(key_of[0], (N_COL, N_ROW * SA, BS, BS), BS ** -0.5, 0.5, ((0, 16), (1, 8)))
    a_rows = draw_a_rows(jax.random.fold_in(key_of[7], 71), 0)
    b_blocks = bell_draw(key_of[2], (N_ROW, N_COL * SBH, BS, BS), 1.0, 6.0, ((0, 8), (1, 16)))
    b_cols = draw_b_cols(jax.random.fold_in(key_of[7], 71), 0)
    c_keep = draw_c_keep(jax.random.fold_in(key_of[7], 71), 0)
    c_owner = draw_c_owner(jax.random.fold_in(key_of[7], 71), 0)
    c_slot = draw_c_slot(jax.random.fold_in(key_of[7], 71), 0)
    return dict(a_blocks=a_blocks, a_rows=a_rows, b_blocks=b_blocks, b_cols=b_cols, c_keep=c_keep, c_owner=c_owner, c_slot=c_slot)


def region_products(a_panel, row_ids, b_panel, col_ids, panel_width, region_size):
    block_size = a_panel.shape[-1]
    left_blocks = a_panel.reshape(panel_width, -1, block_size, block_size).astype(jnp.float32)
    right_blocks = b_panel.reshape(panel_width, -1, block_size, block_size).astype(jnp.float32)
    products = jnp.einsum("kaxy,kbyz->kabxz", left_blocks, right_blocks)
    targets = row_ids.reshape(panel_width, -1)[:, :, None] * panel_width + col_ids.reshape(panel_width, -1)[:, None, :]
    return jax.ops.segment_sum(products.reshape(-1, block_size, block_size), targets.reshape(-1).astype(jnp.int32), num_segments=region_size)


def reference(a_blocks, a_rows, b_blocks, b_cols, c_keep, c_owner, c_slot):
    device_count = N_ROW * N_COL

    def one_device(device_index):
        zero = jnp.zeros((), jnp.int32)
        grid_row = (device_index // N_COL).astype(jnp.int32)
        grid_col = (device_index % N_COL).astype(jnp.int32)
        accumulated = jnp.zeros((RB * CB, BS, BS), jnp.float32)
        for panel_index in range(N_ROW):
            a_source = ((panel_index - grid_col) % N_ROW).astype(jnp.int32)
            b_source = ((panel_index - grid_row) % N_ROW).astype(jnp.int32)
            a_start = (a_source * SA).astype(jnp.int32)
            b_first = (b_source * SBH).astype(jnp.int32)
            b_second = ((b_source + N_ROW) * SBH).astype(jnp.int32)
            a_panel = lax.dynamic_slice(a_blocks, (grid_col, a_start, zero, zero), (1, SA, BS, BS))[0]
            a_index = lax.dynamic_slice(a_rows, (grid_col, a_start), (1, SA))[0]
            first_half = lax.dynamic_slice(b_blocks, (grid_row, b_first, zero, zero), (1, SBH, BS, BS))[0]
            second_half = lax.dynamic_slice(b_blocks, (grid_row, b_second, zero, zero), (1, SBH, BS, BS))[0]
            first_cols = lax.dynamic_slice(b_cols, (grid_row, b_first), (1, SBH))[0]
            second_cols = lax.dynamic_slice(b_cols, (grid_row, b_second), (1, SBH))[0]
            b_panel = jnp.concatenate([first_half, second_half], axis=0)
            b_index = jnp.concatenate([first_cols, second_cols], axis=0)
            accumulated = accumulated + region_products(a_panel, a_index, b_panel, b_index, CB, RB * CB)
        keep_list = c_keep[grid_row, grid_col]
        return accumulated[keep_list].astype(jnp.bfloat16)

    kept_blocks = lax.map(one_device, jnp.arange(device_count, dtype=jnp.int32))
    targets = (c_owner * RCAP + c_slot).reshape(-1).astype(jnp.int32)
    owned_blocks = jnp.zeros((device_count * RCAP, BS, BS), kept_blocks.dtype)
    owned_blocks = owned_blocks.at[targets].set(kept_blocks.reshape(-1, BS, BS))
    return owned_blocks.reshape(N_ROW, N_COL * RCAP, BS, BS)
```

```python
import functools
import itertools
import random

import jax
import jax.numpy as jnp
from jax import lax
from jax.experimental import pallas as pl
from jax.experimental.pallas import tpu as pltpu
from jax.sharding import PartitionSpec as P

MESH = pl.DeviceIdType.MESH
ROWS, COLS = 8, 16
DEVICES = ROWS * COLS
PER_K = 2
PAIR = 2
LANES = 128
FIRST = 22


def coordinates():
    i, j = lax.axis_index("row"), lax.axis_index("col")
    return i // 2, i % 2, j // 4, (j // 2) % 2, j % 2


def device(y, xl, z, xh, core):
    return (y * 2 + xl, (z * 2 + xh) * 2 + core)


def greet(devices):
    barrier = pltpu.get_barrier_semaphore()
    for other in devices:
        pl.semaphore_signal(barrier, inc=1, device_id=other, device_id_type=MESH)
    pl.semaphore_wait(barrier, len(devices))


def gather_kernel(sa, sb, a, b, info, all_a, all_b, row_info, col_info, send_sem, recv_sem, local_sem):
    y, xl, z, xh, core = coordinates()
    i, j = y * 2 + xl, (z * 2 + xh) * 2 + core
    y_next, y_last, y_far = (y + 1) % 4, (y + 3) % 4, (y + 2) % 4
    z_next, z_last, z_far = (z + 1) % 4, (z + 3) % 4, (z + 2) % 4
    xl_other, xh_other = 1 - xl, 1 - xh
    up, down = device(y_next, xl, z, xh, core), device(y_last, xl, z, xh, core)
    ahead, behind = device(y, xl, z_next, xh, core), device(y, xl, z_last, xh, core)
    side, across = device(y, xl_other, z, xh, core), device(y, xl, z, xh_other, core)
    sibling = device(y, xl, z, xh, 1 - core)
    row_mates = [((i + d) % ROWS, j) for d in range(1, ROWS)]
    col_mates = [(i, (j + d) % COLS) for d in range(1, COLS)]
    greet(row_mates + col_mates)

    def in_a(yy, xx, lo, hi):
        return all_a.at[pl.ds((yy * 2 + xx) * sa + lo, hi - lo)]

    def in_b(zz, hh, lo, hi):
        return all_b.at[pl.ds(((zz * 2 + hh) * 2 + core) * sb + lo, hi - lo)]

    copies = {}

    def send(name, src, dst, to):
        k = len(copies)
        copies[name] = pltpu.make_async_remote_copy(
            src_ref=src,
            dst_ref=dst,
            send_sem=send_sem.at[k],
            recv_sem=recv_sem.at[k],
            device_id=to,
            device_id_type=MESH,
        )
        copies[name].start()

    def pass_on(name, block, to):
        send(name, block, block, to)

    def arrived(name):
        copies[name].wait_recv()

    half_a, half_b, half_first = sa // 2, sb // 2, FIRST // 2
    send("a_side", a.at[pl.ds(0, FIRST)], in_a(y, xl, 0, FIRST), side)
    send("a_up", a, in_a(y, xl, 0, sa), up)
    send("a_down", a, in_a(y, xl, 0, sa), down)
    send("b_ahead", b, in_b(z, xh, 0, sb), ahead)
    send("b_behind", b, in_b(z, xh, 0, sb), behind)
    send("b_across", b, in_b(z, xh, 0, sb), across)
    send("a_side_rest", a.at[pl.ds(FIRST, sa - FIRST)], in_a(y, xl, FIRST, sa), side)
    send("b_sibling", b, in_b(z, xh, 0, sb), sibling)
    for d, mate in enumerate(row_mates):
        send(("row", d), info, row_info.at[i], mate)
    for d, mate in enumerate(col_mates):
        send(("col", d), info, col_info.at[j], mate)
    local = [
        pltpu.make_async_copy(a, in_a(y, xl, 0, sa), local_sem.at[0]),
        pltpu.make_async_copy(b, in_b(z, xh, 0, sb), local_sem.at[1]),
        pltpu.make_async_copy(info, row_info.at[i], local_sem.at[2]),
        pltpu.make_async_copy(info, col_info.at[j], local_sem.at[3]),
    ]
    for copy in local:
        copy.start()

    arrived("b_ahead")
    pass_on("b_last_ahead", in_b(z_last, xh, 0, half_b), ahead)
    pass_on("b_last_sibling", in_b(z_last, xh, 0, sb), sibling)
    arrived("b_behind")
    pass_on("b_next_behind", in_b(z_next, xh, half_b, sb), behind)
    pass_on("b_next_sibling", in_b(z_next, xh, 0, sb), sibling)
    arrived("a_side")
    pass_on("a_side_up", in_a(y, xl_other, 0, FIRST), up)
    pass_on("a_side_down", in_a(y, xl_other, 0, FIRST), down)
    arrived("b_across")
    pass_on("b_across_ahead", in_b(z, xh_other, 0, sb), ahead)
    pass_on("b_across_behind", in_b(z, xh_other, 0, sb), behind)
    pass_on("b_across_sibling", in_b(z, xh_other, 0, sb), sibling)
    arrived("a_up")
    pass_on("a_last_up", in_a(y_last, xl, 0, half_a), up)
    pass_on("a_last_side", in_a(y_last, xl, FIRST, sa), side)
    arrived("a_down")
    pass_on("a_next_down", in_a(y_next, xl, half_a, sa), down)
    pass_on("a_next_side", in_a(y_next, xl, FIRST, sa), side)
    arrived("b_last_ahead")
    arrived("b_next_behind")
    pass_on("b_far_sibling", in_b(z_far, xh, 0, sb), sibling)
    arrived("b_across_ahead")
    pass_on("b_across_last_ahead", in_b(z_last, xh_other, 0, half_b), ahead)
    pass_on("b_across_last_sibling", in_b(z_last, xh_other, 0, sb), sibling)
    arrived("b_across_behind")
    pass_on("b_across_next_behind", in_b(z_next, xh_other, half_b, sb), behind)
    pass_on("b_across_next_sibling", in_b(z_next, xh_other, 0, sb), sibling)
    arrived("a_side_up")
    pass_on("a_side_last_up", in_a(y_last, xl_other, 0, half_first), up)
    arrived("a_side_down")
    pass_on("a_side_next_down", in_a(y_next, xl_other, half_first, FIRST), down)
    arrived("a_last_up")
    arrived("a_next_down")
    pass_on("a_far_side", in_a(y_far, xl, FIRST, sa), side)
    arrived("b_across_last_ahead")
    arrived("b_across_next_behind")
    pass_on("b_across_far_sibling", in_b(z_far, xh_other, 0, sb), sibling)
    for name in (
        "a_side_rest", "a_last_side", "a_next_side", "a_side_last_up", "a_side_next_down", "a_far_side",
        "b_sibling", "b_last_sibling", "b_next_sibling", "b_across_sibling", "b_far_sibling",
        "b_across_last_sibling", "b_across_next_sibling", "b_across_far_sibling",
    ):
        arrived(name)
    for d in range(ROWS - 1):
        arrived(("row", d))
    for d in range(COLS - 1):
        arrived(("col", d))
    for copy in copies.values():
        copy.wait_send()
    for copy in local:
        copy.wait()


def gather_panels(a, b, info):
    sa, sb = a.shape[0], b.shape[0]
    block = a.shape[1:]
    messages = 30 + ROWS - 1 + COLS - 1
    anywhere = pl.BlockSpec(memory_space=pl.ANY)
    return pl.pallas_call(
        functools.partial(gather_kernel, sa, sb),
        out_shape=(
            jax.ShapeDtypeStruct((ROWS * sa,) + block, a.dtype),
            jax.ShapeDtypeStruct((COLS * sb,) + block, b.dtype),
            jax.ShapeDtypeStruct((ROWS, 1, LANES), jnp.int32),
            jax.ShapeDtypeStruct((COLS, 1, LANES), jnp.int32),
        ),
        in_specs=[anywhere] * 3,
        out_specs=[anywhere] * 4,
        scratch_shapes=[
            pltpu.SemaphoreType.DMA((messages,)),
            pltpu.SemaphoreType.DMA((messages,)),
            pltpu.SemaphoreType.DMA((4,)),
        ],
        compiler_params=pltpu.CompilerParams(collective_id=0, has_side_effects=True),
        name="gather_panels",
    )(a, b, info)


def multiply_kernel(
    sa, sb, row_info, col_info, keep, place, all_a, all_b, packed, a_buf, b_buf, total, staged, a_sem, b_sem, out_sem
):
    i, j = lax.axis_index("row"), lax.axis_index("col")
    width = sa // PER_K
    half = sb // PER_K

    def fetch_a(s):
        at = pl.ds(s * sa, sa)
        return pltpu.make_async_copy(all_a.at[at], a_buf.at[at], a_sem.at[s])

    def fetch_b(s):
        at = pl.ds(s * sb, sb)
        return pltpu.make_async_copy(all_b.at[at], b_buf.at[at], b_sem.at[s])

    def b_source(s):
        return (s + j + COLS - i) % ROWS

    @pl.loop(0, ROWS)
    def _(s):
        fetch_a(s).start()
        fetch_b(b_source(s)).start()
        fetch_b(b_source(s) + ROWS).start()

    @pl.loop(0, total.shape[0])
    def _(e):
        total[e] = jnp.zeros(total.shape[1:], jnp.float32)

    @pl.loop(0, ROWS)
    def _(s):
        fetch_a(s).wait()
        for h in range(2):
            source = b_source(s) + ROWS * h
            fetch_b(source).wait()

            @pl.loop(0, half // 4)
            def _(quarter):
                for step in range(4):
                    k = quarter * 4 + step
                    a_slot = (h * half + k) * PER_K
                    b_slot = k * PER_K
                    left = a_buf[pl.ds(s * sa + a_slot, PER_K)].reshape(PER_K * LANES, LANES)
                    right = [b_buf[source * sb + b_slot + n] for n in range(PER_K)]
                    products = [jnp.dot(left, r, preferred_element_type=jnp.float32) for r in right]
                    for m in range(PER_K):
                        row = row_info[s, 0, a_slot + m]
                        for n in range(PER_K):
                            col = col_info[source, 0, sa + b_slot + n]
                            total[row * width + col] += products[n][m * LANES : (m + 1) * LANES]

    out = []
    kept = staged.shape[0]

    @pl.loop(0, kept)
    def _(q):
        staged[q] = total[keep[q]].astype(staged.dtype)
        pltpu.make_async_copy(staged.at[q], packed.at[place[q]], out_sem).start()

    pltpu.make_async_copy(staged, packed.at[pl.ds(0, kept)], out_sem).wait()


def multiply(row_info, col_info, keep, place, all_a, all_b):
    sa, sb = all_a.shape[0] // ROWS, all_b.shape[0] // COLS
    block = all_a.shape[1:]
    region = 8 * (sa // PER_K)
    scalars = pl.BlockSpec(memory_space=pltpu.SMEM)
    anywhere = pl.BlockSpec(memory_space=pl.ANY)
    return pl.pallas_call(
        functools.partial(multiply_kernel, sa, sb),
        out_shape=jax.ShapeDtypeStruct((PAIR * DEVICES,) + block, all_a.dtype),
        in_specs=[scalars] * 4 + [anywhere] * 2,
        out_specs=anywhere,
        scratch_shapes=[
            pltpu.VMEM(all_a.shape, all_a.dtype),
            pltpu.VMEM(all_b.shape, all_b.dtype),
            pltpu.VMEM((region,) + block, jnp.float32),
            pltpu.VMEM((keep.shape[0],) + block, all_a.dtype),
            pltpu.SemaphoreType.DMA((ROWS,)),
            pltpu.SemaphoreType.DMA((COLS,)),
            pltpu.SemaphoreType.DMA,
        ],
        compiler_params=pltpu.CompilerParams(vmem_limit_bytes=48 * 1024 * 1024),
        name="multiply",
    )(row_info, col_info, keep, place, all_a, all_b)


def offsets():
    every = [o for o in itertools.product(range(4), range(4), range(4), range(2)) if any(o)]
    random.Random(1).shuffle(every)
    return every


def exchange_kernel(blocks, slots, got_blocks, got_slots, send_sem, recv_sem, slot_send_sem, slot_recv_sem, local_sem):
    y, xl, z, xh, core = coordinates()
    x = xh * 2 + xl
    i, j = y * 2 + xl, (z * 2 + xh) * 2 + core
    me = i * COLS + j
    sign = 1 - 2 * core

    def peer(offset):
        dx, dy, dz, dc = offset
        xx = (x + 4 + sign * dx) % 4
        return device((y + 4 + sign * dy) % 4, xx % 2, (z + 4 + sign * dz) % 4, xx // 2, (core + dc) % 2)

    barrier = pltpu.get_barrier_semaphore()

    @pl.loop(1, DEVICES)
    def _(o):
        xx = (x + o // 2) % 4
        other = device((y + o // 8) % 4, xx % 2, (z + o // 32) % 4, xx // 2, (core + o) % 2)
        pl.semaphore_signal(barrier, inc=1, device_id=other, device_id_type=MESH)

    pl.semaphore_wait(barrier, DEVICES - 1)
    mine = pl.ds(PAIR * me, PAIR)
    for offset in offsets():
        other = peer(offset)
        t = other[0] * COLS + other[1]
        pltpu.make_async_remote_copy(
            src_ref=blocks.at[pl.ds(PAIR * t, PAIR)],
            dst_ref=got_blocks.at[mine],
            send_sem=send_sem,
            recv_sem=recv_sem,
            device_id=other,
            device_id_type=MESH,
        ).start()
        pltpu.make_async_remote_copy(
            src_ref=slots.at[t],
            dst_ref=got_slots.at[me],
            send_sem=slot_send_sem,
            recv_sem=slot_recv_sem,
            device_id=other,
            device_id_type=MESH,
        ).start()
    local = [
        pltpu.make_async_copy(blocks.at[mine], got_blocks.at[mine], local_sem.at[0]),
        pltpu.make_async_copy(slots.at[me], got_slots.at[me], local_sem.at[1]),
    ]
    for copy in local:
        copy.start()
    for copy in local:
        copy.wait()
    others = pl.ds(0, PAIR * (DEVICES - 1))
    every = pltpu.make_async_remote_copy(
        src_ref=blocks.at[others],
        dst_ref=got_blocks.at[others],
        send_sem=send_sem,
        recv_sem=recv_sem,
        device_id=peer((0, 0, 0, 1)),
        device_id_type=MESH,
    )
    every.wait_recv()
    every.wait_send()
    others = pl.ds(0, DEVICES - 1)
    every = pltpu.make_async_remote_copy(
        src_ref=slots.at[others],
        dst_ref=got_slots.at[others],
        send_sem=slot_send_sem,
        recv_sem=slot_recv_sem,
        device_id=peer((0, 0, 0, 1)),
        device_id_type=MESH,
    )
    every.wait_recv()
    every.wait_send()


def exchange(blocks, slots):
    anywhere = pl.BlockSpec(memory_space=pl.ANY)
    return pl.pallas_call(
        exchange_kernel,
        out_shape=(
            jax.ShapeDtypeStruct(blocks.shape, blocks.dtype),
            jax.ShapeDtypeStruct(slots.shape, slots.dtype),
        ),
        in_specs=[anywhere] * 2,
        out_specs=[anywhere] * 2,
        scratch_shapes=[pltpu.SemaphoreType.DMA] * 4 + [pltpu.SemaphoreType.DMA((2,))],
        compiler_params=pltpu.CompilerParams(collective_id=1, has_side_effects=True),
        name="exchange",
    )(blocks, slots)


def place_kernel(slots, blocks, owned, zero, filled, sem):
    capacity = owned.shape[0]
    zero[...] = jnp.zeros(zero.shape, zero.dtype)

    @pl.loop(0, capacity)
    def _(s):
        filled[s] = 0

    @pl.loop(0, blocks.shape[0] // PAIR)
    def _(source):
        for member in range(PAIR):
            slot = slots[source, 0, member]

            @pl.when(slot < capacity)
            def _():
                filled[slot] = 1
                pltpu.make_async_copy(blocks.at[source * PAIR + member], owned.at[slot], sem).start()

    @pl.loop(0, capacity)
    def _(s):
        @pl.when(filled[s] == 0)
        def _():
            pltpu.make_async_copy(zero, owned.at[s], sem).start()

    pltpu.make_async_copy(owned, owned, sem).wait()


def place_blocks(slots, blocks, capacity):
    block = blocks.shape[1:]
    return pl.pallas_call(
        place_kernel,
        out_shape=jax.ShapeDtypeStruct((capacity,) + block, blocks.dtype),
        in_specs=[pl.BlockSpec(memory_space=pltpu.SMEM), pl.BlockSpec(memory_space=pl.ANY)],
        out_specs=pl.BlockSpec(memory_space=pl.ANY),
        scratch_shapes=[
            pltpu.VMEM(block, blocks.dtype),
            pltpu.SMEM((capacity,), jnp.int32),
            pltpu.SemaphoreType.DMA,
        ],
        name="place",
    )(slots, blocks)


def body(a_blocks, a_rows, b_blocks, b_cols, c_keep, c_owner, c_slot):
    capacity = PAIR * DEVICES
    sa, sb = a_rows.shape[1], b_cols.shape[1]
    info = jnp.concatenate([a_rows, b_cols, jnp.zeros((1, LANES - sa - sb), jnp.int32)], axis=1)
    keep, owner, slot = c_keep[0, 0], c_owner[0, 0], c_slot[0, 0]
    count = jnp.arange(keep.shape[0], dtype=jnp.int32)
    earlier = (owner[:, None] == owner[None, :]) & (count[None, :] < count[:, None])
    place = owner * PAIR + jnp.sum(earlier.astype(jnp.int32), axis=1)
    target = jnp.arange(DEVICES, dtype=jnp.int32)[:, None, None] * PAIR + jnp.arange(PAIR, dtype=jnp.int32)[None, :, None]
    hit = target == place[None, None, :]
    slots = capacity + jnp.sum(jnp.where(hit, slot[None, None, :] - capacity, 0), axis=2)
    slots = jnp.pad(slots, ((0, 0), (0, LANES - PAIR)))[:, None, :]
    all_a, all_b, row_info, col_info = gather_panels(a_blocks[0], b_blocks[0], info)
    packed = multiply(row_info, col_info, keep, place, all_a, all_b)
    got_blocks, got_slots = exchange(packed, slots)
    return place_blocks(got_slots, got_blocks, capacity)[None]


def solution(mesh):
    return jax.shard_map(
        body,
        mesh=mesh,
        in_specs=(
            P("col", "row", None, None),
            P("col", "row"),
            P("row", "col", None, None),
            P("row", "col"),
            P("row", "col", None),
            P("row", "col", None),
            P("row", "col", None),
        ),
        out_specs=P("row", "col", None, None),
        check_vma=False,
    )
```

```python
import functools
import itertools
import random

import jax
import jax.numpy as jnp
from jax import lax
from jax.experimental import pallas as pl
from jax.experimental.pallas import tpu as pltpu
from jax.sharding import PartitionSpec as P

MESH = pl.DeviceIdType.MESH
ROWS, COLS = 8, 16
DEVICES = ROWS * COLS
PER_K = 2
PAIR = 2
LANES = 128
FIRST = 22


def coordinates():
    i, j = lax.axis_index("row"), lax.axis_index("col")
    return i // 2, i % 2, j // 4, (j // 2) % 2, j % 2


def device(y, xl, z, xh, core):
    return (y * 2 + xl, (z * 2 + xh) * 2 + core)


def greet(devices):
    barrier = pltpu.get_barrier_semaphore()
    for other in devices:
        pl.semaphore_signal(barrier, inc=1, device_id=other, device_id_type=MESH)
    pl.semaphore_wait(barrier, len(devices))


def gather_kernel(sa, sb, a, b, info, all_a, all_b, row_info, col_info, send_sem, recv_sem, local_sem):
    y, xl, z, xh, core = coordinates()
    i, j = y * 2 + xl, (z * 2 + xh) * 2 + core
    y_next, y_last, y_far = (y + 1) % 4, (y + 3) % 4, (y + 2) % 4
    z_next, z_last, z_far = (z + 1) % 4, (z + 3) % 4, (z + 2) % 4
    xl_other, xh_other = 1 - xl, 1 - xh
    up, down = device(y_next, xl, z, xh, core), device(y_last, xl, z, xh, core)
    ahead, behind = device(y, xl, z_next, xh, core), device(y, xl, z_last, xh, core)
    side, across = device(y, xl_other, z, xh, core), device(y, xl, z, xh_other, core)
    sibling = device(y, xl, z, xh, 1 - core)
    row_mates = [((i + d) % ROWS, j) for d in range(1, ROWS)]
    col_mates = [(i, (j + d) % COLS) for d in range(1, COLS)]
    greet(row_mates + col_mates)

    def in_a(yy, xx, lo, hi):
        return all_a.at[pl.ds((yy * 2 + xx) * sa + lo, hi - lo)]

    def in_b(zz, hh, lo, hi):
        return all_b.at[pl.ds(((zz * 2 + hh) * 2 + core) * sb + lo, hi - lo)]

    copies = {}

    def send(name, src, dst, to):
        k = len(copies)
        copies[name] = pltpu.make_async_remote_copy(
            src_ref=src,
            dst_ref=dst,
            send_sem=send_sem.at[k],
            recv_sem=recv_sem.at[k],
            device_id=to,
            device_id_type=MESH,
        )
        copies[name].start()

    def pass_on(name, block, to):
        send(name, block, block, to)

    def arrived(name):
        copies[name].wait_recv()

    half_a, half_b, half_first = sa // 2, sb // 2, FIRST // 2
    send("a_side", a.at[pl.ds(0, FIRST)], in_a(y, xl, 0, FIRST), side)
    send("a_up", a, in_a(y, xl, 0, sa), up)
    send("a_down", a, in_a(y, xl, 0, sa), down)
    send("b_ahead", b, in_b(z, xh, 0, sb), ahead)
    send("b_behind", b, in_b(z, xh, 0, sb), behind)
    send("b_across", b, in_b(z, xh, 0, sb), across)
    send("a_side_rest", a.at[pl.ds(FIRST, sa - FIRST)], in_a(y, xl, FIRST, sa), side)
    send("b_sibling", b, in_b(z, xh, 0, sb), sibling)
    for d, mate in enumerate(row_mates):
        send(("row", d), info, row_info.at[i], mate)
    for d, mate in enumerate(col_mates):
        send(("col", d), info, col_info.at[j], mate)
    local = [
        pltpu.make_async_copy(a, in_a(y, xl, 0, sa), local_sem.at[0]),
        pltpu.make_async_copy(b, in_b(z, xh, 0, sb), local_sem.at[1]),
        pltpu.make_async_copy(info, row_info.at[i], local_sem.at[2]),
        pltpu.make_async_copy(info, col_info.at[j], local_sem.at[3]),
    ]
    for copy in local:
        copy.start()

    arrived("b_ahead")
    pass_on("b_last_ahead", in_b(z_last, xh, 0, half_b), ahead)
    pass_on("b_last_sibling", in_b(z_last, xh, 0, sb), sibling)
    arrived("b_behind")
    pass_on("b_next_behind", in_b(z_next, xh, half_b, sb), behind)
    pass_on("b_next_sibling", in_b(z_next, xh, 0, sb), sibling)
    arrived("a_side")
    pass_on("a_side_up", in_a(y, xl_other, 0, FIRST), up)
    pass_on("a_side_down", in_a(y, xl_other, 0, FIRST), down)
    arrived("b_across")
    pass_on("b_across_ahead", in_b(z, xh_other, 0, sb), ahead)
    pass_on("b_across_behind", in_b(z, xh_other, 0, sb), behind)
    pass_on("b_across_sibling", in_b(z, xh_other, 0, sb), sibling)
    arrived("a_up")
    pass_on("a_last_up", in_a(y_last, xl, 0, half_a), up)
    pass_on("a_last_side", in_a(y_last, xl, FIRST, sa), side)
    arrived("a_down")
    pass_on("a_next_down", in_a(y_next, xl, half_a, sa), down)
    pass_on("a_next_side", in_a(y_next, xl, FIRST, sa), side)
    arrived("b_last_ahead")
    arrived("b_next_behind")
    pass_on("b_far_sibling", in_b(z_far, xh, 0, sb), sibling)
    arrived("b_across_ahead")
    pass_on("b_across_last_ahead", in_b(z_last, xh_other, 0, half_b), ahead)
    pass_on("b_across_last_sibling", in_b(z_last, xh_other, 0, sb), sibling)
    arrived("b_across_behind")
    pass_on("b_across_next_behind", in_b(z_next, xh_other, half_b, sb), behind)
    pass_on("b_across_next_sibling", in_b(z_next, xh_other, 0, sb), sibling)
    arrived("a_side_up")
    pass_on("a_side_last_up", in_a(y_last, xl_other, 0, half_first), up)
    arrived("a_side_down")
    pass_on("a_side_next_down", in_a(y_next, xl_other, half_first, FIRST), down)
    arrived("a_last_up")
    arrived("a_next_down")
    pass_on("a_far_side", in_a(y_far, xl, FIRST, sa), side)
    arrived("b_across_last_ahead")
    arrived("b_across_next_behind")
    pass_on("b_across_far_sibling", in_b(z_far, xh_other, 0, sb), sibling)
    for name in (
        "a_side_rest", "a_last_side", "a_next_side", "a_side_last_up", "a_side_next_down", "a_far_side",
        "b_sibling", "b_last_sibling", "b_next_sibling", "b_across_sibling", "b_far_sibling",
        "b_across_last_sibling", "b_across_next_sibling", "b_across_far_sibling",
    ):
        arrived(name)
    for d in range(ROWS - 1):
        arrived(("row", d))
    for d in range(COLS - 1):
        arrived(("col", d))
    for copy in copies.values():
        copy.wait_send()
    for copy in local:
        copy.wait()


def gather_panels(a, b, info):
    sa, sb = a.shape[0], b.shape[0]
    block = a.shape[1:]
    messages = 30 + ROWS - 1 + COLS - 1
    anywhere = pl.BlockSpec(memory_space=pl.ANY)
    return pl.pallas_call(
        functools.partial(gather_kernel, sa, sb),
        out_shape=(
            jax.ShapeDtypeStruct((ROWS * sa,) + block, a.dtype),
            jax.ShapeDtypeStruct((COLS * sb,) + block, b.dtype),
            jax.ShapeDtypeStruct((ROWS, 1, LANES), jnp.int32),
            jax.ShapeDtypeStruct((COLS, 1, LANES), jnp.int32),
        ),
        in_specs=[anywhere] * 3,
        out_specs=[anywhere] * 4,
        scratch_shapes=[
            pltpu.SemaphoreType.DMA((messages,)),
            pltpu.SemaphoreType.DMA((messages,)),
            pltpu.SemaphoreType.DMA((4,)),
        ],
        compiler_params=pltpu.CompilerParams(collective_id=0, has_side_effects=True),
        name="gather_panels",
    )(a, b, info)


def multiply_kernel(
    sa, sb, row_info, col_info, keep, place, all_a, all_b, packed, a_buf, b_buf, total, staged, a_sem, b_sem, out_sem
):
    i, j = lax.axis_index("row"), lax.axis_index("col")
    width = sa // PER_K
    half = sb // PER_K

    def fetch_a(s):
        at = pl.ds(s * sa, sa)
        return pltpu.make_async_copy(all_a.at[at], a_buf.at[at], a_sem.at[s])

    def fetch_b(s):
        at = pl.ds(s * sb, sb)
        return pltpu.make_async_copy(all_b.at[at], b_buf.at[at], b_sem.at[s])

    def b_source(s):
        return (s + j + COLS - i) % ROWS

    @pl.loop(0, ROWS)
    def _(s):
        fetch_a(s).start()
        fetch_b(b_source(s)).start()
        fetch_b(b_source(s) + ROWS).start()

    @pl.loop(0, total.shape[0])
    def _(e):
        total[e] = jnp.zeros(total.shape[1:], jnp.float32)

    @pl.loop(0, ROWS)
    def _(s):
        fetch_a(s).wait()
        for h in range(2):
            source = b_source(s) + ROWS * h
            fetch_b(source).wait()

            @pl.loop(0, half // 4)
            def _(quarter):
                for step in range(4):
                    k = quarter * 4 + step
                    a_slot = (h * half + k) * PER_K
                    b_slot = k * PER_K
                    left = a_buf[pl.ds(s * sa + a_slot, PER_K)].reshape(PER_K * LANES, LANES)
                    right = [b_buf[source * sb + b_slot + n] for n in range(PER_K)]
                    products = [jnp.dot(left, r, preferred_element_type=jnp.float32) for r in right]
                    for m in range(PER_K):
                        row = row_info[s, 0, a_slot + m]
                        for n in range(PER_K):
                            col = col_info[source, 0, sa + b_slot + n]
                            total[row * width + col] += products[n][m * LANES : (m + 1) * LANES]

    out = []
    kept = staged.shape[0]

    @pl.loop(0, kept)
    def _(q):
        staged[q] = total[keep[q]].astype(staged.dtype)
        pltpu.make_async_copy(staged.at[q], packed.at[place[q]], out_sem).start()

    pltpu.make_async_copy(staged, packed.at[pl.ds(0, kept)], out_sem).wait()


def multiply(row_info, col_info, keep, place, all_a, all_b):
    sa, sb = all_a.shape[0] // ROWS, all_b.shape[0] // COLS
    block = all_a.shape[1:]
    region = 8 * (sa // PER_K)
    scalars = pl.BlockSpec(memory_space=pltpu.SMEM)
    anywhere = pl.BlockSpec(memory_space=pl.ANY)
    return pl.pallas_call(
        functools.partial(multiply_kernel, sa, sb),
        out_shape=jax.ShapeDtypeStruct((PAIR * DEVICES,) + block, all_a.dtype),
        in_specs=[scalars] * 4 + [anywhere] * 2,
        out_specs=anywhere,
        scratch_shapes=[
            pltpu.VMEM(all_a.shape, all_a.dtype),
            pltpu.VMEM(all_b.shape, all_b.dtype),
            pltpu.VMEM((region,) + block, jnp.float32),
            pltpu.VMEM((keep.shape[0],) + block, all_a.dtype),
            pltpu.SemaphoreType.DMA((ROWS,)),
            pltpu.SemaphoreType.DMA((COLS,)),
            pltpu.SemaphoreType.DMA,
        ],
        compiler_params=pltpu.CompilerParams(vmem_limit_bytes=48 * 1024 * 1024),
        name="multiply",
    )(row_info, col_info, keep, place, all_a, all_b)


def offsets():
    every = [o for o in itertools.product(range(4), range(4), range(4), range(2)) if any(o)]
    random.Random(1).shuffle(every)
    return every


def exchange_kernel(blocks, slots, got_blocks, got_slots, send_sem, recv_sem, slot_send_sem, slot_recv_sem, local_sem):
    y, xl, z, xh, core = coordinates()
    x = xh * 2 + xl
    i, j = y * 2 + xl, (z * 2 + xh) * 2 + core
    me = i * COLS + j
    sign = 1 - 2 * core

    def peer(offset):
        dx, dy, dz, dc = offset
        xx = (x + 4 + sign * dx) % 4
        return device((y + 4 + sign * dy) % 4, xx % 2, (z + 4 + sign * dz) % 4, xx // 2, (core + dc) % 2)

    barrier = pltpu.get_barrier_semaphore()

    @pl.loop(1, DEVICES)
    def _(o):
        xx = (x + o // 2) % 4
        other = device((y + o // 8) % 4, xx % 2, (z + o // 32) % 4, xx // 2, (core + o) % 2)
        pl.semaphore_signal(barrier, inc=1, device_id=other, device_id_type=MESH)

    pl.semaphore_wait(barrier, DEVICES - 1)
    mine = pl.ds(PAIR * me, PAIR)
    for offset in offsets():
        other = peer(offset)
        t = other[0] * COLS + other[1]
        pltpu.make_async_remote_copy(
            src_ref=blocks.at[pl.ds(PAIR * t, PAIR)],
            dst_ref=got_blocks.at[mine],
            send_sem=send_sem,
            recv_sem=recv_sem,
            device_id=other,
            device_id_type=MESH,
        ).start()
        pltpu.make_async_remote_copy(
            src_ref=slots.at[t],
            dst_ref=got_slots.at[me],
            send_sem=slot_send_sem,
            recv_sem=slot_recv_sem,
            device_id=other,
            device_id_type=MESH,
        ).start()
    local = [
        pltpu.make_async_copy(blocks.at[mine], got_blocks.at[mine], local_sem.at[0]),
        pltpu.make_async_copy(slots.at[me], got_slots.at[me], local_sem.at[1]),
    ]
    for copy in local:
        copy.start()
    for copy in local:
        copy.wait()
    others = pl.ds(0, PAIR * (DEVICES - 1))
    every = pltpu.make_async_remote_copy(
        src_ref=blocks.at[others],
        dst_ref=got_blocks.at[others],
        send_sem=send_sem,
        recv_sem=recv_sem,
        device_id=peer((0, 0, 0, 1)),
        device_id_type=MESH,
    )
    every.wait_recv()
    every.wait_send()
    others = pl.ds(0, DEVICES - 1)
    every = pltpu.make_async_remote_copy(
        src_ref=slots.at[others],
        dst_ref=got_slots.at[others],
        send_sem=slot_send_sem,
        recv_sem=slot_recv_sem,
        device_id=peer((0, 0, 0, 1)),
        device_id_type=MESH,
    )
    every.wait_recv()
    every.wait_send()


def exchange(blocks, slots):
    anywhere = pl.BlockSpec(memory_space=pl.ANY)
    return pl.pallas_call(
        exchange_kernel,
        out_shape=(
            jax.ShapeDtypeStruct(blocks.shape, blocks.dtype),
            jax.ShapeDtypeStruct(slots.shape, slots.dtype),
        ),
        in_specs=[anywhere] * 2,
        out_specs=[anywhere] * 2,
        scratch_shapes=[pltpu.SemaphoreType.DMA] * 4 + [pltpu.SemaphoreType.DMA((2,))],
        compiler_params=pltpu.CompilerParams(collective_id=1, has_side_effects=True),
        name="exchange",
    )(blocks, slots)


def place_kernel(slots, blocks, owned, held, zero, filled, load_sem, sem):
    capacity = owned.shape[0]
    parts = load_sem.shape[0]
    size = blocks.shape[0] // parts

    def load(part):
        at = pl.ds(part * size, size)
        return pltpu.make_async_copy(blocks.at[at], held.at[at], load_sem.at[part])

    @pl.loop(0, parts)
    def _(part):
        load(part).start()

    zero[...] = jnp.zeros(zero.shape, zero.dtype)

    @pl.loop(0, capacity, unroll=8)
    def _(s):
        filled[s] = 0

    @pl.loop(0, blocks.shape[0] // PAIR, unroll=4)
    def _(source):
        for member in range(PAIR):
            filled[slots[source, 0, member]] = 1

    @pl.loop(0, parts)
    def _(part):
        load(part).wait()

        @pl.loop(part * size // PAIR, (part + 1) * size // PAIR)
        def _(source):
            for member in range(PAIR):
                slot = slots[source, 0, member]

                @pl.when(slot < capacity)
                def _():
                    pltpu.make_async_copy(held.at[source * PAIR + member], owned.at[slot], sem).start()

    @pl.loop(0, capacity)
    def _(s):
        @pl.when(filled[s] == 0)
        def _():
            pltpu.make_async_copy(zero, owned.at[s], sem).start()

    pltpu.make_async_copy(held, owned, sem).wait()


def place_blocks(slots, blocks, capacity):
    block = blocks.shape[1:]
    return pl.pallas_call(
        place_kernel,
        out_shape=jax.ShapeDtypeStruct((capacity,) + block, blocks.dtype),
        in_specs=[pl.BlockSpec(memory_space=pltpu.SMEM), pl.BlockSpec(memory_space=pl.ANY)],
        out_specs=pl.BlockSpec(memory_space=pl.ANY),
        scratch_shapes=[
            pltpu.VMEM(blocks.shape, blocks.dtype),
            pltpu.VMEM(block, blocks.dtype),
            pltpu.SMEM((capacity + 1,), jnp.int32),
            pltpu.SemaphoreType.DMA((16,)),
            pltpu.SemaphoreType.DMA,
        ],
        compiler_params=pltpu.CompilerParams(vmem_limit_bytes=24 * 1024 * 1024),
        name="place",
    )(slots, blocks)


def body(a_blocks, a_rows, b_blocks, b_cols, c_keep, c_owner, c_slot):
    capacity = PAIR * DEVICES
    sa, sb = a_rows.shape[1], b_cols.shape[1]
    info = jnp.concatenate([a_rows, b_cols, jnp.zeros((1, LANES - sa - sb), jnp.int32)], axis=1)
    keep, owner, slot = c_keep[0, 0], c_owner[0, 0], c_slot[0, 0]
    count = jnp.arange(keep.shape[0], dtype=jnp.int32)
    earlier = (owner[:, None] == owner[None, :]) & (count[None, :] < count[:, None])
    place = owner * PAIR + jnp.sum(earlier.astype(jnp.int32), axis=1)
    target = jnp.arange(DEVICES, dtype=jnp.int32)[:, None, None] * PAIR + jnp.arange(PAIR, dtype=jnp.int32)[None, :, None]
    hit = target == place[None, None, :]
    slots = capacity + jnp.sum(jnp.where(hit, slot[None, None, :] - capacity, 0), axis=2)
    slots = jnp.pad(slots, ((0, 0), (0, LANES - PAIR)))[:, None, :]
    all_a, all_b, row_info, col_info = gather_panels(a_blocks[0], b_blocks[0], info)
    packed = multiply(row_info, col_info, keep, place, all_a, all_b)
    got_blocks, got_slots = exchange(packed, slots)
    return place_blocks(got_slots, got_blocks, capacity)[None]


def solution(mesh):
    return jax.shard_map(
        body,
        mesh=mesh,
        in_specs=(
            P("col", "row", None, None),
            P("col", "row"),
            P("row", "col", None, None),
            P("row", "col"),
            P("row", "col", None),
            P("row", "col", None),
            P("row", "col", None),
        ),
        out_specs=P("row", "col", None, None),
        check_vma=False,
    )
```

```python
import functools
import itertools
import random

import jax
import jax.numpy as jnp
from jax import lax
from jax.experimental import pallas as pl
from jax.experimental.pallas import tpu as pltpu
from jax.sharding import PartitionSpec as P

MESH = pl.DeviceIdType.MESH
ROWS, COLS = 8, 16
DEVICES = ROWS * COLS
PER_K = 2
PAIR = 2
LANES = 128
FIRST = 22
SLOTS = PAIR * DEVICES
PACK = 512


def coordinates():
    i, j = lax.axis_index("row"), lax.axis_index("col")
    return i // 2, i % 2, j // 4, (j // 2) % 2, j % 2


def device(y, xl, z, xh, core):
    return (y * 2 + xl, (z * 2 + xh) * 2 + core)


def offsets():
    every = [o for o in itertools.product(range(4), range(4), range(4), range(2)) if any(o)]
    random.Random(1).shuffle(every)
    return every


def iota(axis):
    return lax.broadcasted_iota(jnp.int32, (LANES, LANES), axis)


def column(row):
    return jnp.sum(jnp.where(iota(0) == iota(1), row, 0), axis=1, keepdims=True)


def count(mask, axis):
    return jnp.sum(mask.astype(jnp.int32), axis=axis, keepdims=True)


def pick(mask, values):
    return jnp.sum(jnp.where(mask, values, 0), axis=0, keepdims=True)


def combine_kernel(
    sa, sb, a, b, a_rows, b_cols, keep, owner, slot, got_blocks, got_slots,
    panels, products, packed, raw, row_info, col_info, slot_info, table, index,
    send_sem, recv_sem, local_sem, ready, block_send, block_recv, slot_send, slot_recv,
):
    y, xl, z, xh, core = coordinates()
    x = xh * 2 + xl
    i, j = y * 2 + xl, (z * 2 + xh) * 2 + core
    me = i * COLS + j
    width = sa // PER_K
    per_panel = width * PER_K * PER_K
    b_start = ROWS * sa
    y_next, y_last, y_far = (y + 1) % 4, (y + 3) % 4, (y + 2) % 4
    z_next, z_last, z_far = (z + 1) % 4, (z + 3) % 4, (z + 2) % 4
    xl_other, xh_other = 1 - xl, 1 - xh
    up, down = device(y_next, xl, z, xh, core), device(y_last, xl, z, xh, core)
    ahead, behind = device(y, xl, z_next, xh, core), device(y, xl, z_last, xh, core)
    side, across = device(y, xl_other, z, xh, core), device(y, xl, z, xh_other, core)
    sibling = device(y, xl, z, xh, 1 - core)
    row_mates = [((i + d) % ROWS, j) for d in range(1, ROWS)]
    col_mates = [(i, (j + d) % COLS) for d in range(1, COLS)]

    barrier = pltpu.get_barrier_semaphore()
    for mate in row_mates + col_mates:
        pl.semaphore_signal(barrier, inc=1, device_id=mate, device_id_type=MESH)
    pl.semaphore_wait(barrier, ROWS + COLS - 2)

    def in_a(yy, xx, lo, hi):
        return panels.at[pl.ds((yy * 2 + xx) * sa + lo, hi - lo)]

    def in_b(zz, hh, lo, hi):
        return panels.at[pl.ds(b_start + ((zz * 2 + hh) * 2 + core) * sb + lo, hi - lo)]

    copies = {}

    def send(name, src, dst, to):
        k = len(copies)
        copies[name] = pltpu.make_async_remote_copy(
            src_ref=src,
            dst_ref=dst,
            send_sem=send_sem.at[k],
            recv_sem=recv_sem.at[k],
            device_id=to,
            device_id_type=MESH,
        )
        copies[name].start()

    def pass_on(name, block, to):
        send(name, block, block, to)

    def arrived(*names):
        for name in names:
            copies[name].wait_recv()

    half_a, half_b, half_first = sa // 2, sb // 2, FIRST // 2
    send("a_side", a.at[pl.ds(0, FIRST)], in_a(y, xl, 0, FIRST), side)
    send("a_up", a, in_a(y, xl, 0, sa), up)
    send("a_down", a, in_a(y, xl, 0, sa), down)
    send("b_ahead", b, in_b(z, xh, 0, sb), ahead)
    send("b_behind", b, in_b(z, xh, 0, sb), behind)
    send("b_sibling", b, in_b(z, xh, 0, sb), sibling)
    local_a = pltpu.make_async_copy(a, in_a(y, xl, 0, sa), local_sem.at[0])
    local_b = pltpu.make_async_copy(b, in_b(z, xh, 0, sb), local_sem.at[1])
    local_a.start()
    local_b.start()

    sub, lane = iota(0), iota(1)
    lane_row = lane[0:1]
    raw[...] = jnp.full(raw.shape, -1, jnp.int32)
    raw[0:1, 0:sa] = a_rows[...]
    raw[1:2, 0:sb] = b_cols[...]
    raw[2:3, 0 : keep.shape[1]] = keep[...]
    raw[3:4, 0 : owner.shape[1]] = owner[...]
    raw[4:5, 0 : slot.shape[1]] = slot[...]
    within = lane % per_panel
    a_lanes = pick(sub == (within // 4) * 2 + (within // 2) % 2, column(raw[0:1]) * width)
    row_info[i] = jnp.where(lane_row // per_panel == i % 2, a_lanes, 0)
    of_half = within - (per_panel // 2) * (j // ROWS)
    b_lanes = pick((sub == (of_half // 4) * 2 + of_half % 2) & (of_half >= 0) & (of_half < per_panel // 2), column(raw[1:2]))
    col_info[j] = b_lanes
    for d, mate in enumerate(row_mates):
        pass_on(("row", d), row_info.at[i], mate)
    for d, mate in enumerate(col_mates):
        pass_on(("col", d), col_info.at[j], mate)

    keep_col, owner_row, owner_col, slot_col = column(raw[2:3]), raw[3:4], column(raw[3:4]), column(raw[4:5])
    earlier = count((owner_col == owner_row) & (lane < sub), 1)
    place_col = jnp.where(owner_col >= 0, owner_col * PAIR + earlier, -1)
    slot_info[...] = SLOTS * (1 + PACK) + pick(
        owner_col == lane, (slot_col - SLOTS) * jnp.where(earlier == 0, 1, PACK)
    )

    for d in range(ROWS - 1):
        arrived(("row", d))
    for d in range(COLS - 1):
        arrived(("col", d))
    for mate in row_mates:
        pl.semaphore_signal(ready, inc=1, device_id=mate, device_id_type=MESH)

    def b_source(s):
        return (s + j + COLS - i) % ROWS

    def b_targets(s):
        return col_info[b_source(s)] + col_info[b_source(s) + ROWS]

    groups = ROWS // 2
    target_row = [
        row_info[2 * g] + row_info[2 * g + 1] + jnp.where(lane_row < per_panel, b_targets(2 * g), b_targets(2 * g + 1))
        for g in range(groups)
    ]
    target_col = [column(row) for row in target_row]
    rank, first = [], []
    for u in range(groups):
        before = jnp.zeros((LANES, LANES), jnp.int32)
        same = jnp.zeros((LANES, LANES), jnp.int32)
        for v in range(groups):
            lower = target_row[v] < target_col[u]
            equal = target_row[v] == target_col[u]
            if v == u:
                equal = equal & (lane < sub)
            if v <= u:
                before += (lower | equal).astype(jnp.int32)
                same += equal.astype(jnp.int32)
            else:
                before += lower.astype(jnp.int32)
        rank.append(jnp.sum(before, axis=1, keepdims=True))
        first.append((jnp.sum(same, axis=1, keepdims=True) == 0).astype(jnp.int32))
    for w in range(groups):
        here = [rank[u] == w * LANES + lane for u in range(groups)]
        table[w : w + 1] = sum(pick(here[u], u * LANES + sub) for u in range(groups))
        table[groups + w : groups + w + 1] = sum(pick(here[u], first[u]) for u in range(groups))
    for w in range(SLOTS // LANES):
        kept = pick(place_col == w * LANES + lane, keep_col + 1) - 1
        upto = sum(count(target_col[u] <= kept, 0) for u in range(groups))
        equal = sum(count(target_col[u] == kept, 0) for u in range(groups))
        table[8 + w : 9 + w] = jnp.maximum(upto - 1, 0)
        table[10 + w : 11 + w] = (equal > 0).astype(jnp.int32)
    to_scalars = pltpu.make_async_copy(table, index, local_sem.at[2])
    to_scalars.start()

    def multiply(yy, xx):
        s = yy * 2 + xx
        for h in range(2):
            source = b_source(s) + ROWS * h

            @pl.loop(0, width // 2 // 4)
            def _(quarter):
                for step in range(4):
                    k = quarter * 4 + step
                    left = panels[pl.ds(s * sa + (h * width // 2 + k) * PER_K, PER_K)].reshape(PER_K * LANES, LANES)
                    at = s * per_panel + (h * width // 2 + k) * PER_K * PER_K
                    for n in range(PER_K):
                        right = panels[b_start + source * sb + k * PER_K + n]
                        out = jnp.dot(left, right, preferred_element_type=jnp.float32)
                        for m in range(PER_K):
                            products[at + m * PER_K + n] = out[m * LANES : (m + 1) * LANES]

    arrived("b_ahead")
    pass_on("b_last_ahead", in_b(z_last, xh, 0, half_b), ahead)
    pass_on("b_last_sibling", in_b(z_last, xh, 0, sb), sibling)
    arrived("b_behind")
    pass_on("b_next_behind", in_b(z_next, xh, half_b, sb), behind)
    pass_on("b_next_sibling", in_b(z_next, xh, 0, sb), sibling)
    arrived("a_side")
    pass_on("a_side_up", in_a(y, xl_other, 0, FIRST), up)
    pass_on("a_side_down", in_a(y, xl_other, 0, FIRST), down)
    send("b_across", b, in_b(z, xh, 0, sb), across)
    send("a_side_rest", a.at[pl.ds(FIRST, sa - FIRST)], in_a(y, xl, FIRST, sa), side)

    def peer(offset, sign):
        dx, dy, dz, dc = offset
        xx = (x + 4 + sign * dx) % 4
        return device((y + 4 + sign * dy) % 4, xx % 2, (z + 4 + sign * dz) % 4, xx // 2, (core + dc) % 2)

    pl.semaphore_wait(ready, ROWS - 1)

    @pl.loop(1, DEVICES)
    def _(o):
        pltpu.make_async_remote_copy(
            src_ref=slot_info,
            dst_ref=got_slots.at[me],
            send_sem=slot_send,
            recv_sem=slot_recv,
            device_id=peer((o // 2, o // 8, o // 32, o), 1),
            device_id_type=MESH,
        ).start()

    local_slots = pltpu.make_async_copy(slot_info, got_slots.at[me], local_sem.at[3])
    local_slots.start()

    arrived("b_last_ahead", "b_next_behind")
    pass_on("b_far_sibling", in_b(z_far, xh, 0, sb), sibling)
    arrived("a_up")
    pass_on("a_last_up", in_a(y_last, xl, 0, half_a), up)
    pass_on("a_last_side", in_a(y_last, xl, FIRST, sa), side)
    arrived("a_down")
    pass_on("a_next_down", in_a(y_next, xl, half_a, sa), down)
    pass_on("a_next_side", in_a(y_next, xl, FIRST, sa), side)
    arrived("b_across")
    pass_on("b_across_ahead", in_b(z, xh_other, 0, sb), ahead)
    pass_on("b_across_behind", in_b(z, xh_other, 0, sb), behind)
    pass_on("b_across_sibling", in_b(z, xh_other, 0, sb), sibling)
    arrived("b_across_ahead")
    pass_on("b_across_last_ahead", in_b(z_last, xh_other, 0, half_b), ahead)
    pass_on("b_across_last_sibling", in_b(z_last, xh_other, 0, sb), sibling)
    arrived("b_across_behind")
    pass_on("b_across_next_behind", in_b(z_next, xh_other, half_b, sb), behind)
    pass_on("b_across_next_sibling", in_b(z_next, xh_other, 0, sb), sibling)
    arrived("a_side_up")
    pass_on("a_side_last_up", in_a(y_last, xl_other, 0, half_first), up)
    arrived("a_side_down")
    pass_on("a_side_next_down", in_a(y_next, xl_other, half_first, FIRST), down)
    arrived("b_across_last_ahead", "b_across_next_behind")
    pass_on("b_across_far_sibling", in_b(z_far, xh_other, 0, sb), sibling)
    arrived(
        "b_sibling", "b_last_sibling", "b_next_sibling", "b_across_sibling", "b_far_sibling",
        "b_across_last_sibling", "b_across_next_sibling", "b_across_far_sibling",
    )
    local_a.wait()
    local_b.wait()
    multiply(y, xl)
    multiply(y_last, xl)
    multiply(y_next, xl)
    arrived("a_last_up", "a_next_down")
    pass_on("a_far_side", in_a(y_far, xl, FIRST, sa), side)
    multiply(y_far, xl)
    arrived("a_side_rest")
    multiply(y, xl_other)
    arrived("a_last_side")
    multiply(y_last, xl_other)
    arrived("a_next_side")
    multiply(y_next, xl_other)
    arrived("a_side_last_up", "a_side_next_down", "a_far_side")
    multiply(y_far, xl_other)
    for copy in copies.values():
        copy.wait_send()
    to_scalars.wait()

    def add(r, total):
        product = products[index[r // LANES, r % LANES]]
        total = jnp.where(index[groups + r // LANES, r % LANES] > 0, product, total + product)
        panels[r] = total.astype(panels.dtype)
        return total

    lax.fori_loop(0, groups * LANES, add, jnp.zeros((LANES, LANES), jnp.float32), unroll=4)

    def pack(t):
        for member in range(PAIR):
            at = PAIR * t + member
            block = panels[index[8 + at // LANES, at % LANES]]
            packed[at] = jnp.where(index[10 + at // LANES, at % LANES] > 0, block, jnp.zeros_like(block))

    for offset in offsets():
        other = peer(offset, 1 - 2 * core)
        t = other[0] * COLS + other[1]
        pack(t)
        pltpu.make_async_remote_copy(
            src_ref=packed.at[pl.ds(PAIR * t, PAIR)],
            dst_ref=got_blocks.at[pl.ds(PAIR * me, PAIR)],
            send_sem=block_send,
            recv_sem=block_recv,
            device_id=other,
            device_id_type=MESH,
        ).start()
    pack(me)
    mine = pl.ds(PAIR * me, PAIR)
    local_blocks = pltpu.make_async_copy(packed.at[mine], got_blocks.at[mine], local_sem.at[4])
    local_blocks.start()

    others = pl.ds(0, DEVICES - 1)
    every_slot = pltpu.make_async_remote_copy(
        src_ref=got_slots.at[others],
        dst_ref=got_slots.at[others],
        send_sem=slot_send,
        recv_sem=slot_recv,
        device_id=sibling,
        device_id_type=MESH,
    )
    every_slot.wait_recv()
    every_slot.wait_send()
    others = pl.ds(0, PAIR * (DEVICES - 1))
    every_block = pltpu.make_async_remote_copy(
        src_ref=packed.at[others],
        dst_ref=got_blocks.at[others],
        send_sem=block_send,
        recv_sem=block_recv,
        device_id=sibling,
        device_id_type=MESH,
    )
    every_block.wait_recv()
    every_block.wait_send()
    local_slots.wait()
    local_blocks.wait()


def combine(a, b, a_rows, b_cols, keep, owner, slot):
    sa, sb = a.shape[0], b.shape[0]
    block = a.shape[1:]
    panel_blocks = ROWS * sa + COLS * sb
    product_count = ROWS * (sa // PER_K) * PER_K * PER_K
    messages = 34 + ROWS - 1 + COLS - 1
    anywhere = pl.BlockSpec(memory_space=pl.ANY)
    vmem = pl.BlockSpec(memory_space=pltpu.VMEM)
    return pl.pallas_call(
        functools.partial(combine_kernel, sa, sb),
        out_shape=(
            jax.ShapeDtypeStruct((SLOTS,) + block, a.dtype),
            jax.ShapeDtypeStruct((DEVICES, 1, LANES), jnp.int32),
        ),
        in_specs=[anywhere] * 2 + [vmem] * 5,
        out_specs=[anywhere] * 2,
        scratch_shapes=[
            pltpu.VMEM((panel_blocks,) + block, a.dtype),
            pltpu.VMEM((product_count,) + block, jnp.float32),
            pltpu.VMEM((SLOTS,) + block, a.dtype),
            pltpu.VMEM((8, LANES), jnp.int32),
            pltpu.VMEM((ROWS, 1, LANES), jnp.int32),
            pltpu.VMEM((COLS, 1, LANES), jnp.int32),
            pltpu.VMEM((1, LANES), jnp.int32),
            pltpu.VMEM((16, LANES), jnp.int32),
            pltpu.SMEM((16, LANES), jnp.int32),
            pltpu.SemaphoreType.DMA((messages,)),
            pltpu.SemaphoreType.DMA((messages,)),
            pltpu.SemaphoreType.DMA((5,)),
            pltpu.SemaphoreType.REGULAR,
            pltpu.SemaphoreType.DMA,
            pltpu.SemaphoreType.DMA,
            pltpu.SemaphoreType.DMA,
            pltpu.SemaphoreType.DMA,
        ],
        compiler_params=pltpu.CompilerParams(
            collective_id=0, has_side_effects=True, vmem_limit_bytes=62 * 1024 * 1024
        ),
        name="combine",
    )(a, b, a_rows, b_cols, keep, owner, slot)


def place_kernel(slots, blocks, owned, held, zero, filled, load_sem, sem):
    capacity = owned.shape[0]
    parts = load_sem.shape[0]
    size = blocks.shape[0] // parts

    me = lax.axis_index("row") * COLS + lax.axis_index("col")

    def slot_of(source, member):
        both = slots[source, 0, me]
        return both // PACK if member else both % PACK

    def load(part):
        at = pl.ds(part * size, size)
        return pltpu.make_async_copy(blocks.at[at], held.at[at], load_sem.at[part])

    @pl.loop(0, parts)
    def _(part):
        load(part).start()

    zero[...] = jnp.zeros(zero.shape, zero.dtype)

    @pl.loop(0, capacity, unroll=8)
    def _(s):
        filled[s] = 0

    @pl.loop(0, blocks.shape[0] // PAIR, unroll=4)
    def _(source):
        for member in range(PAIR):
            filled[slot_of(source, member)] = 1

    @pl.loop(0, parts)
    def _(part):
        load(part).wait()

        @pl.loop(part * size // PAIR, (part + 1) * size // PAIR)
        def _(source):
            for member in range(PAIR):
                slot = slot_of(source, member)

                @pl.when(slot < capacity)
                def _():
                    pltpu.make_async_copy(held.at[source * PAIR + member], owned.at[slot], sem).start()

    @pl.loop(0, capacity)
    def _(s):
        @pl.when(filled[s] == 0)
        def _():
            pltpu.make_async_copy(zero, owned.at[s], sem).start()

    pltpu.make_async_copy(held, owned, sem).wait()


def place_blocks(slots, blocks, capacity):
    block = blocks.shape[1:]
    return pl.pallas_call(
        place_kernel,
        out_shape=jax.ShapeDtypeStruct((capacity,) + block, blocks.dtype),
        in_specs=[pl.BlockSpec(memory_space=pltpu.SMEM), pl.BlockSpec(memory_space=pl.ANY)],
        out_specs=pl.BlockSpec(memory_space=pl.ANY),
        scratch_shapes=[
            pltpu.VMEM(blocks.shape, blocks.dtype),
            pltpu.VMEM(block, blocks.dtype),
            pltpu.SMEM((capacity + 1,), jnp.int32),
            pltpu.SemaphoreType.DMA((16,)),
            pltpu.SemaphoreType.DMA,
        ],
        compiler_params=pltpu.CompilerParams(vmem_limit_bytes=56 * 1024 * 1024),
        name="place",
    )(slots, blocks)


def body(a_blocks, a_rows, b_blocks, b_cols, c_keep, c_owner, c_slot):
    got_blocks, got_slots = combine(a_blocks[0], b_blocks[0], a_rows, b_cols, c_keep[0], c_owner[0], c_slot[0])
    return place_blocks(got_slots, got_blocks, SLOTS)[None]


def solution(mesh):
    return jax.shard_map(
        body,
        mesh=mesh,
        in_specs=(
            P("col", "row", None, None),
            P("col", "row"),
            P("row", "col", None, None),
            P("row", "col"),
            P("row", "col", None),
            P("row", "col", None),
            P("row", "col", None),
        ),
        out_specs=P("row", "col", None, None),
        check_vma=False,
    )
```

```python
import functools
import itertools
import random

import jax
import jax.numpy as jnp
from jax import lax
from jax.experimental import pallas as pl
from jax.experimental.pallas import tpu as pltpu
from jax.sharding import PartitionSpec as P

MESH = pl.DeviceIdType.MESH
ROWS, COLS = 8, 16
DEVICES = ROWS * COLS
PER_K = 2
PAIR = 2
LANES = 128
FIRST = 22
SLOTS = PAIR * DEVICES
PACK = 512


def coordinates():
    i, j = lax.axis_index("row"), lax.axis_index("col")
    return i // 2, i % 2, j // 4, (j // 2) % 2, j % 2


def device(y, xl, z, xh, core):
    return (y * 2 + xl, (z * 2 + xh) * 2 + core)


def offsets():
    every = [o for o in itertools.product(range(4), range(4), range(4), range(2)) if any(o)]
    random.Random(1).shuffle(every)
    return every


def iota(axis):
    return lax.broadcasted_iota(jnp.int32, (LANES, LANES), axis)


def column(row):
    return jnp.sum(jnp.where(iota(0) == iota(1), row, 0), axis=1, keepdims=True)


def column_of(values, at):
    return jnp.sum(jnp.where(iota(1) == at, values, 0), axis=1, keepdims=True)


def count(mask, axis):
    return jnp.sum(mask.astype(jnp.int32), axis=axis, keepdims=True)


def pick(mask, values):
    return jnp.sum(jnp.where(mask, values, 0), axis=0, keepdims=True)


def combine_kernel(
    sa, sb, a, b, a_rows, b_cols, keep, owner, slot, got_blocks, places,
    panels, products, packed, raw, row_info, col_info, slot_info, got_slots, table, index,
    send_sem, recv_sem, local_sem, ready, block_send, block_recv, slot_send, slot_recv,
):
    y, xl, z, xh, core = coordinates()
    x = xh * 2 + xl
    i, j = y * 2 + xl, (z * 2 + xh) * 2 + core
    me = i * COLS + j
    width = sa // PER_K
    per_panel = width * PER_K * PER_K
    b_start = ROWS * sa
    y_next, y_last, y_far = (y + 1) % 4, (y + 3) % 4, (y + 2) % 4
    z_next, z_last, z_far = (z + 1) % 4, (z + 3) % 4, (z + 2) % 4
    xl_other, xh_other = 1 - xl, 1 - xh
    up, down = device(y_next, xl, z, xh, core), device(y_last, xl, z, xh, core)
    ahead, behind = device(y, xl, z_next, xh, core), device(y, xl, z_last, xh, core)
    side, across = device(y, xl_other, z, xh, core), device(y, xl, z, xh_other, core)
    sibling = device(y, xl, z, xh, 1 - core)
    row_mates = [((i + d) % ROWS, j) for d in range(1, ROWS)]
    col_mates = [(i, (j + d) % COLS) for d in range(1, COLS)]

    barrier = pltpu.get_barrier_semaphore()
    for mate in row_mates + col_mates:
        pl.semaphore_signal(barrier, inc=1, device_id=mate, device_id_type=MESH)
    sub, lane = iota(0), iota(1)
    lane_row = lane[0:1]
    raw[...] = jnp.full(raw.shape, -1, jnp.int32)
    raw[0:1, 0:sa] = a_rows[...]
    raw[1:2, 0:sb] = b_cols[...]
    raw[2:3, 0 : keep.shape[1]] = keep[...]
    raw[3:4, 0 : owner.shape[1]] = owner[...]
    raw[4:5, 0 : slot.shape[1]] = slot[...]
    within = lane % per_panel
    a_lanes = pick(sub == (within // 4) * 2 + (within // 2) % 2, column(raw[0:1]) * width)
    row_info[i] = jnp.where(lane_row // per_panel == i % 2, a_lanes, 0)
    of_half = within - (per_panel // 2) * (j // ROWS)
    b_lanes = pick((sub == (of_half // 4) * 2 + of_half % 2) & (of_half >= 0) & (of_half < per_panel // 2), column(raw[1:2]))
    col_info[j] = b_lanes
    pl.semaphore_wait(barrier, ROWS + COLS - 2)

    def in_a(yy, xx, lo, hi):
        return panels.at[pl.ds((yy * 2 + xx) * sa + lo, hi - lo)]

    def in_b(zz, hh, lo, hi):
        return panels.at[pl.ds(b_start + ((zz * 2 + hh) * 2 + core) * sb + lo, hi - lo)]

    copies = {}

    def send(name, src, dst, to):
        k = len(copies)
        copies[name] = pltpu.make_async_remote_copy(
            src_ref=src,
            dst_ref=dst,
            send_sem=send_sem.at[k],
            recv_sem=recv_sem.at[k],
            device_id=to,
            device_id_type=MESH,
        )
        copies[name].start()

    def pass_on(name, block, to):
        send(name, block, block, to)

    def arrived(*names):
        for name in names:
            copies[name].wait_recv()

    half_a, half_b, half_first = sa // 2, sb // 2, FIRST // 2
    for d, mate in enumerate(row_mates):
        pass_on(("row", d), row_info.at[i], mate)
    for d, mate in enumerate(col_mates):
        pass_on(("col", d), col_info.at[j], mate)
    send("a_side_0", a.at[pl.ds(0, half_first)], in_a(y, xl, 0, half_first), side)
    send("a_up_0", a.at[pl.ds(0, half_a)], in_a(y, xl, 0, half_a), up)
    send("a_down_1", a.at[pl.ds(half_a, half_a)], in_a(y, xl, half_a, sa), down)
    send("b_ahead", b, in_b(z, xh, 0, sb), ahead)
    send("b_behind", b, in_b(z, xh, 0, sb), behind)
    send("b_across", b, in_b(z, xh, 0, sb), across)
    send("a_up_1", a.at[pl.ds(half_a, half_a)], in_a(y, xl, half_a, sa), up)
    send("a_down_0", a.at[pl.ds(0, half_a)], in_a(y, xl, 0, half_a), down)
    send("a_side_1", a.at[pl.ds(half_first, half_first)], in_a(y, xl, half_first, FIRST), side)
    send("a_side_rest", a.at[pl.ds(FIRST, sa - FIRST)], in_a(y, xl, FIRST, sa), side)
    send("b_sibling", b, in_b(z, xh, 0, sb), sibling)
    local_a = pltpu.make_async_copy(a, in_a(y, xl, 0, sa), local_sem.at[0])
    local_b = pltpu.make_async_copy(b, in_b(z, xh, 0, sb), local_sem.at[1])
    local_a.start()
    local_b.start()

    def multiply(yy, xx):
        s = yy * 2 + xx
        for h in range(2):
            source = b_source(s) + ROWS * h

            @pl.loop(0, width // 2 // 4)
            def _(quarter):
                for step in range(4):
                    k = quarter * 4 + step
                    left = panels[pl.ds(s * sa + (h * width // 2 + k) * PER_K, PER_K)].reshape(PER_K * LANES, LANES)
                    at = s * per_panel + (h * width // 2 + k) * PER_K * PER_K
                    for n in range(PER_K):
                        right = panels[b_start + source * sb + k * PER_K + n]
                        out = jnp.dot(left, right, preferred_element_type=jnp.float32)
                        for m in range(PER_K):
                            products[at + m * PER_K + n] = out[m * LANES : (m + 1) * LANES]

    def peer(offset, sign):
        dx, dy, dz, dc = offset
        xx = (x + 4 + sign * dx) % 4
        return device((y + 4 + sign * dy) % 4, xx % 2, (z + 4 + sign * dz) % 4, xx // 2, (core + dc) % 2)

    arrived("b_ahead")
    pass_on("b_last_ahead", in_b(z_last, xh, 0, half_b), ahead)
    pass_on("b_last_sibling", in_b(z_last, xh, 0, sb), sibling)
    arrived("b_behind")
    pass_on("b_next_behind", in_b(z_next, xh, half_b, sb), behind)
    pass_on("b_next_sibling", in_b(z_next, xh, 0, sb), sibling)

    keep_col, owner_row, owner_col, slot_col = column(raw[2:3]), raw[3:4], column(raw[3:4]), column(raw[4:5])
    earlier = count((owner_col == owner_row) & (lane < sub), 1)
    place_col = jnp.where(owner_col >= 0, owner_col * PAIR + earlier, -1)
    slot_info[...] = SLOTS * (1 + PACK) + pick(
        owner_col == lane, (slot_col - SLOTS) * jnp.where(earlier == 0, 1, PACK)
    )

    for d in range(ROWS - 1):
        arrived(("row", d))
    for d in range(COLS - 1):
        arrived(("col", d))
    for mate in row_mates:
        pl.semaphore_signal(ready, inc=1, device_id=mate, device_id_type=MESH)

    def b_source(s):
        return (s + j + COLS - i) % ROWS

    def b_targets(s):
        return col_info[b_source(s)] + col_info[b_source(s) + ROWS]

    groups = ROWS // 2
    target_row = [
        row_info[2 * g] + row_info[2 * g + 1] + jnp.where(lane_row < per_panel, b_targets(2 * g), b_targets(2 * g + 1))
        for g in range(groups)
    ]
    target_col = [column(row) for row in target_row]
    rank, first = [], []
    for u in range(groups):
        before = jnp.zeros((LANES, LANES), jnp.int32)
        same = jnp.zeros((LANES, LANES), jnp.int32)
        for v in range(groups):
            lower = target_row[v] < target_col[u]
            equal = target_row[v] == target_col[u]
            if v == u:
                equal = equal & (lane < sub)
            if v <= u:
                before += (lower | equal).astype(jnp.int32)
                same += equal.astype(jnp.int32)
            else:
                before += lower.astype(jnp.int32)
        rank.append(jnp.sum(before, axis=1, keepdims=True))
        first.append((jnp.sum(same, axis=1, keepdims=True) == 0).astype(jnp.int32))
    for w in range(groups):
        here = [rank[u] == w * LANES + lane for u in range(groups)]
        table[w : w + 1] = sum(pick(here[u], u * LANES + sub) for u in range(groups))
        table[groups + w : groups + w + 1] = sum(pick(here[u], first[u]) for u in range(groups))
    for w in range(SLOTS // LANES):
        kept = pick(place_col == w * LANES + lane, keep_col + 1) - 1
        upto = sum(count(target_col[u] <= kept, 0) for u in range(groups))
        equal = sum(count(target_col[u] == kept, 0) for u in range(groups))
        table[8 + w : 9 + w] = jnp.maximum(upto - 1, 0)
        table[10 + w : 11 + w] = (equal > 0).astype(jnp.int32)
    to_scalars = pltpu.make_async_copy(table, index, local_sem.at[2])
    to_scalars.start()

    arrived("a_up_0")
    pass_on("a_last_up", in_a(y_last, xl, 0, half_a), up)
    arrived("a_down_1")
    pass_on("a_next_down", in_a(y_next, xl, half_a, sa), down)
    arrived("a_side_0")
    pass_on("a_side_up_0", in_a(y, xl_other, 0, half_first), up)
    pass_on("a_side_down_0", in_a(y, xl_other, 0, half_first), down)
    arrived("b_across")
    pass_on("b_across_ahead", in_b(z, xh_other, 0, sb), ahead)
    pass_on("b_across_behind", in_b(z, xh_other, 0, sb), behind)
    pass_on("b_across_sibling", in_b(z, xh_other, 0, sb), sibling)
    arrived("a_up_1")
    pass_on("a_last_side", in_a(y_last, xl, FIRST, sa), side)
    pass_on("a_next_side", in_a(y_next, xl, FIRST, sa), side)
    arrived("a_down_0")
    arrived("a_side_1")
    pass_on("a_side_up_1", in_a(y, xl_other, half_first, FIRST), up)
    pass_on("a_side_down_1", in_a(y, xl_other, half_first, FIRST), down)
    pl.semaphore_wait(ready, ROWS - 1)

    @pl.loop(1, DEVICES)
    def _(o):
        pltpu.make_async_remote_copy(
            src_ref=slot_info,
            dst_ref=got_slots.at[me],
            send_sem=slot_send,
            recv_sem=slot_recv,
            device_id=peer((o // 2, o // 8, o // 32, o), 1),
            device_id_type=MESH,
        ).start()

    local_slots = pltpu.make_async_copy(slot_info, got_slots.at[me], local_sem.at[3])
    local_slots.start()

    arrived("b_last_ahead", "b_next_behind")
    pass_on("b_far_sibling", in_b(z_far, xh, 0, sb), sibling)
    arrived("a_next_down")
    pass_on("a_far_side", in_a(y_far, xl, FIRST, sa), side)
    arrived("b_across_ahead")
    pass_on("b_across_last_ahead", in_b(z_last, xh_other, 0, half_b), ahead)
    pass_on("b_across_last_sibling", in_b(z_last, xh_other, 0, sb), sibling)
    arrived("b_across_behind")
    pass_on("b_across_next_behind", in_b(z_next, xh_other, half_b, sb), behind)
    pass_on("b_across_next_sibling", in_b(z_next, xh_other, 0, sb), sibling)
    arrived("a_side_up_0")
    pass_on("a_side_last_up", in_a(y_last, xl_other, 0, half_first), up)
    arrived("a_side_down_1")
    pass_on("a_side_next_down", in_a(y_next, xl_other, half_first, FIRST), down)
    arrived("b_across_last_ahead", "b_across_next_behind")
    pass_on("b_across_far_sibling", in_b(z_far, xh_other, 0, sb), sibling)
    arrived(
        "b_sibling", "b_last_sibling", "b_next_sibling", "b_across_sibling", "b_far_sibling",
        "b_across_last_sibling", "b_across_next_sibling", "b_across_far_sibling",
    )
    local_a.wait()
    local_b.wait()
    multiply(y, xl)
    multiply(y_last, xl)
    multiply(y_next, xl)
    arrived("a_side_rest")
    multiply(y, xl_other)
    arrived("a_last_up")
    multiply(y_far, xl)
    arrived("a_last_side", "a_side_up_1")
    multiply(y_last, xl_other)
    arrived("a_next_side", "a_side_down_0")
    multiply(y_next, xl_other)
    arrived("a_side_last_up", "a_side_next_down", "a_far_side")
    multiply(y_far, xl_other)
    for copy in copies.values():
        copy.wait_send()
    to_scalars.wait()

    def add(group, r, total):
        product = products[index[group, r]]
        total = jnp.where(index[groups + group, r] > 0, product, total + product)
        panels[group * LANES + r] = total.astype(panels.dtype)
        return total

    total = jnp.zeros((LANES, LANES), jnp.float32)
    for group in range(groups):
        total = lax.fori_loop(0, LANES, functools.partial(add, group), total, unroll=8)

    def pack(at):
        block = panels[index[8 + at // LANES, at % LANES]]
        packed[at] = jnp.where(index[10 + at // LANES, at % LANES] > 0, block, jnp.zeros_like(block))

    @pl.loop(0, PAIR)
    def _(member):
        for offset in offsets():
            other = peer(offset, 1 - 2 * core)
            at = PAIR * (other[0] * COLS + other[1]) + member
            pack(at)
            pltpu.make_async_remote_copy(
                src_ref=packed.at[pl.ds(at, 1)],
                dst_ref=got_blocks.at[pl.ds(PAIR * me + member, 1)],
                send_sem=block_send,
                recv_sem=block_recv,
                device_id=other,
                device_id_type=MESH,
            ).start()
        pack(PAIR * me + member)

    mine = pl.ds(PAIR * me, PAIR)
    local_blocks = pltpu.make_async_copy(packed.at[mine], got_blocks.at[mine], local_sem.at[4])
    local_blocks.start()

    others = pl.ds(0, DEVICES - 1)
    every_slot = pltpu.make_async_remote_copy(
        src_ref=got_slots.at[others],
        dst_ref=got_slots.at[others],
        send_sem=slot_send,
        recv_sem=slot_recv,
        device_id=sibling,
        device_id_type=MESH,
    )
    every_slot.wait_recv()
    every_slot.wait_send()
    local_slots.wait()
    from_all = column_of(got_slots[...].reshape(DEVICES, LANES), me)
    goes = [from_all // PACK if member else from_all % PACK for member in range(PAIR)]
    places[...] = jnp.zeros(places.shape, jnp.int32)
    for w in range(SLOTS // LANES):
        source = sum(pick(goes[member] == w * LANES + lane, PAIR * sub + member - SLOTS) for member in range(PAIR))
        places[w : w + 1] = source + SLOTS
    others = pl.ds(0, PAIR * (DEVICES - 1))
    every_block = pltpu.make_async_remote_copy(
        src_ref=packed.at[others],
        dst_ref=got_blocks.at[others],
        send_sem=block_send,
        recv_sem=block_recv,
        device_id=sibling,
        device_id_type=MESH,
    )
    every_block.wait_recv()
    every_block.wait_send()
    local_blocks.wait()


def combine(a, b, a_rows, b_cols, keep, owner, slot):
    sa, sb = a.shape[0], b.shape[0]
    block = a.shape[1:]
    panel_blocks = ROWS * sa + COLS * sb
    product_count = ROWS * (sa // PER_K) * PER_K * PER_K
    messages = 44 + ROWS - 1 + COLS - 1
    anywhere = pl.BlockSpec(memory_space=pl.ANY)
    vmem = pl.BlockSpec(memory_space=pltpu.VMEM)
    return pl.pallas_call(
        functools.partial(combine_kernel, sa, sb),
        out_shape=(
            jax.ShapeDtypeStruct((SLOTS,) + block, a.dtype),
            jax.ShapeDtypeStruct((8, LANES), jnp.int32),
        ),
        in_specs=[anywhere] * 2 + [vmem] * 5,
        out_specs=[anywhere, vmem],
        scratch_shapes=[
            pltpu.VMEM((panel_blocks,) + block, a.dtype),
            pltpu.VMEM((product_count,) + block, jnp.float32),
            pltpu.VMEM((SLOTS,) + block, a.dtype),
            pltpu.VMEM((8, LANES), jnp.int32),
            pltpu.VMEM((ROWS, 1, LANES), jnp.int32),
            pltpu.VMEM((COLS, 1, LANES), jnp.int32),
            pltpu.VMEM((1, LANES), jnp.int32),
            pltpu.VMEM((DEVICES, 1, LANES), jnp.int32),
            pltpu.VMEM((16, LANES), jnp.int32),
            pltpu.SMEM((16, LANES), jnp.int32),
            pltpu.SemaphoreType.DMA((messages,)),
            pltpu.SemaphoreType.DMA((messages,)),
            pltpu.SemaphoreType.DMA((5,)),
            pltpu.SemaphoreType.REGULAR,
            pltpu.SemaphoreType.DMA,
            pltpu.SemaphoreType.DMA,
            pltpu.SemaphoreType.DMA,
            pltpu.SemaphoreType.DMA,
        ],
        compiler_params=pltpu.CompilerParams(
            collective_id=0, has_side_effects=True, vmem_limit_bytes=62 * 1024 * 1024
        ),
        name="combine",
    )(a, b, a_rows, b_cols, keep, owner, slot)


def place_kernel(places, blocks, owned, held, laid, load_sem, store_sem):
    parts = load_sem.shape[0]
    size = SLOTS // parts

    def load(part):
        at = pl.ds(part * size, size)
        return pltpu.make_async_copy(blocks.at[at], held.at[at], load_sem.at[part])

    def store(part):
        at = pl.ds(part * size, size)
        return pltpu.make_async_copy(laid.at[at], owned.at[at], store_sem.at[part])

    for part in range(parts):
        load(part).start()
    held[SLOTS] = jnp.zeros(held.shape[1:], held.dtype)
    for part in range(parts):
        load(part).wait()
    for part in range(parts):

        @pl.loop(0, size, unroll=4)
        def _(n):
            slot = part * size + n
            laid[slot] = held[places[slot // LANES, slot % LANES]]

        store(part).start()
    for part in range(parts):
        store(part).wait()


def place_blocks(places, blocks):
    block = blocks.shape[1:]
    parts = 8
    return pl.pallas_call(
        place_kernel,
        out_shape=jax.ShapeDtypeStruct(blocks.shape, blocks.dtype),
        in_specs=[pl.BlockSpec(memory_space=pltpu.SMEM), pl.BlockSpec(memory_space=pl.ANY)],
        out_specs=pl.BlockSpec(memory_space=pl.ANY),
        scratch_shapes=[
            pltpu.VMEM((SLOTS + 1,) + block, blocks.dtype),
            pltpu.VMEM((SLOTS,) + block, blocks.dtype),
            pltpu.SemaphoreType.DMA((parts,)),
            pltpu.SemaphoreType.DMA((parts,)),
        ],
        compiler_params=pltpu.CompilerParams(vmem_limit_bytes=56 * 1024 * 1024),
        name="place",
    )(places, blocks)


def body(a_blocks, a_rows, b_blocks, b_cols, c_keep, c_owner, c_slot):
    got_blocks, places = combine(a_blocks[0], b_blocks[0], a_rows, b_cols, c_keep[0], c_owner[0], c_slot[0])
    return place_blocks(places, got_blocks)[None]


def solution(mesh):
    return jax.shard_map(
        body,
        mesh=mesh,
        in_specs=(
            P("col", "row", None, None),
            P("col", "row"),
            P("row", "col", None, None),
            P("row", "col"),
            P("row", "col", None),
            P("row", "col", None),
            P("row", "col", None),
        ),
        out_specs=P("row", "col", None, None),
        check_vma=False,
    )
```

```python
import functools
import itertools
import random

import jax
import jax.numpy as jnp
from jax import lax
from jax.experimental import pallas as pl
from jax.experimental.pallas import tpu as pltpu
from jax.sharding import PartitionSpec as P

MESH = pl.DeviceIdType.MESH
ROWS, COLS = 8, 16
DEVICES = ROWS * COLS
PER_K = 2
PAIR = 2
LANES = 128
FIRST = 22
SLOTS = PAIR * DEVICES
PACK = 512
HALVES = 2


def coordinates():
    i, j = lax.axis_index("row"), lax.axis_index("col")
    return i // 2, i % 2, j // 4, (j // 2) % 2, j % 2


def device(y, xl, z, xh, core):
    return (y * 2 + xl, (z * 2 + xh) * 2 + core)


def offsets():
    every = [o for o in itertools.product(range(4), range(4), range(4), range(2)) if any(o)]
    random.Random(3).shuffle(every)
    return every


def iota(axis):
    return lax.broadcasted_iota(jnp.int32, (LANES, LANES), axis)


def column(row):
    return jnp.sum(jnp.where(iota(0) == iota(1), row, 0), axis=1, keepdims=True)


def column_of(values, at):
    return jnp.sum(jnp.where(iota(1) == at, values, 0), axis=1, keepdims=True)


def count(mask, axis):
    return jnp.sum(mask.astype(jnp.int32), axis=axis, keepdims=True)


def pick(mask, values):
    return jnp.sum(jnp.where(mask, values, 0), axis=0, keepdims=True)


def combine_kernel(
    sa, sb, a, b, a_rows, b_cols, keep, owner, slot, got_blocks, places,
    a_panels, b_panels, products, sums, packed, raw, row_info, col_info, slot_info, got_slots, table, index,
    send_sem, recv_sem, local_sem, ready, block_send, block_recv, slot_send, slot_recv,
):
    y, xl, z, xh, core = coordinates()
    x = xh * 2 + xl
    i, j = y * 2 + xl, (z * 2 + xh) * 2 + core
    me = i * COLS + j
    width = sa // PER_K
    per_panel = width * PER_K * PER_K
    rows = LANES // HALVES
    y_next, y_last, y_far = (y + 1) % 4, (y + 3) % 4, (y + 2) % 4
    z_next, z_last, z_far = (z + 1) % 4, (z + 3) % 4, (z + 2) % 4
    xl_other, xh_other = 1 - xl, 1 - xh
    up, down = device(y_next, xl, z, xh, core), device(y_last, xl, z, xh, core)
    ahead, behind = device(y, xl, z_next, xh, core), device(y, xl, z_last, xh, core)
    side, across = device(y, xl_other, z, xh, core), device(y, xl, z, xh_other, core)
    sibling = device(y, xl, z, xh, 1 - core)
    row_mates = [((i + d) % ROWS, j) for d in range(1, ROWS)]
    col_mates = [(i, (j + d) % COLS) for d in range(1, COLS)]

    barrier = pltpu.get_barrier_semaphore()
    for mate in row_mates + col_mates:
        pl.semaphore_signal(barrier, inc=1, device_id=mate, device_id_type=MESH)
    sub, lane = iota(0), iota(1)
    lane_row = lane[0:1]
    raw[...] = jnp.full(raw.shape, -1, jnp.int32)
    raw[0:1, 0:sa] = a_rows[...]
    raw[1:2, 0:sb] = b_cols[...]
    raw[2:3, 0 : keep.shape[1]] = keep[...]
    raw[3:4, 0 : owner.shape[1]] = owner[...]
    raw[4:5, 0 : slot.shape[1]] = slot[...]
    within = lane % per_panel
    a_lanes = pick(sub == (within // 4) * 2 + (within // 2) % 2, column(raw[0:1]) * width)
    row_info[i] = jnp.where(lane_row // per_panel == i % 2, a_lanes, 0)
    of_half = within - (per_panel // 2) * (j // ROWS)
    b_lanes = pick((sub == (of_half // 4) * 2 + of_half % 2) & (of_half >= 0) & (of_half < per_panel // 2), column(raw[1:2]))
    col_info[j] = b_lanes
    pl.semaphore_wait(barrier, ROWS + COLS - 2)

    def in_a(h, yy, xx, lo, hi):
        return a_panels.at[h, pl.ds((yy * 2 + xx) * sa + lo, hi - lo)]

    def own_a(h, lo, hi):
        return a.at[pl.ds(lo, hi - lo), pl.ds(h * rows, rows)]

    def in_b(zz, hh, lo, hi):
        return b_panels.at[pl.ds(((zz * 2 + hh) * 2 + core) * sb + lo, hi - lo)]

    copies = {}

    def send(name, src, dst, to):
        k = len(copies)
        copies[name] = pltpu.make_async_remote_copy(
            src_ref=src,
            dst_ref=dst,
            send_sem=send_sem.at[k],
            recv_sem=recv_sem.at[k],
            device_id=to,
            device_id_type=MESH,
        )
        copies[name].start()

    def pass_on(name, block, to):
        send(name, block, block, to)

    def arrived(*names):
        for name in names:
            copies[name].wait_recv()

    def arrived_a(h, *names):
        arrived(*((name, h) for name in names))

    half_a, half_b, half_first = sa // 2, sb // 2, FIRST // 2

    def send_own(h):
        send(("side", h), own_a(h, 0, FIRST), in_a(h, y, xl, 0, FIRST), side)
        send(("up", h), own_a(h, 0, sa), in_a(h, y, xl, 0, sa), up)
        send(("down", h), own_a(h, 0, sa), in_a(h, y, xl, 0, sa), down)

    def send_rest(h):
        send(("rest", h), own_a(h, FIRST, sa), in_a(h, y, xl, FIRST, sa), side)

    def forward_near(h):
        arrived_a(h, "up")
        pass_on(("last_up", h), in_a(h, y_last, xl, 0, half_a), up)
        pass_on(("last_side", h), in_a(h, y_last, xl, FIRST, sa), side)
        arrived_a(h, "down")
        pass_on(("next_down", h), in_a(h, y_next, xl, half_a, sa), down)
        pass_on(("next_side", h), in_a(h, y_next, xl, FIRST, sa), side)

    def forward_side(h):
        arrived_a(h, "side")
        pass_on(("side_up", h), in_a(h, y, xl_other, 0, FIRST), up)
        pass_on(("side_down", h), in_a(h, y, xl_other, 0, FIRST), down)

    def forward_far(h):
        arrived_a(h, "next_down")
        pass_on(("far_side", h), in_a(h, y_far, xl, FIRST, sa), side)

    def forward_last(h):
        arrived_a(h, "side_up")
        pass_on(("side_last_up", h), in_a(h, y_last, xl_other, 0, half_first), up)
        arrived_a(h, "side_down")
        pass_on(("side_next_down", h), in_a(h, y_next, xl_other, half_first, FIRST), down)

    for d, mate in enumerate(row_mates):
        pass_on(("row", d), row_info.at[i], mate)
    for d, mate in enumerate(col_mates):
        pass_on(("col", d), col_info.at[j], mate)
    send("b_across_0", b.at[pl.ds(0, half_b)], in_b(z, xh, 0, half_b), across)
    send("b_across_1", b.at[pl.ds(half_b, half_b)], in_b(z, xh, half_b, sb), across)
    send("b_ahead_0", b.at[pl.ds(0, half_b)], in_b(z, xh, 0, half_b), ahead)
    send("b_behind_1", b.at[pl.ds(half_b, half_b)], in_b(z, xh, half_b, sb), behind)
    send(("up", 0), own_a(0, 0, sa), in_a(0, y, xl, 0, sa), up)
    send(("down", 0), own_a(0, 0, sa), in_a(0, y, xl, 0, sa), down)
    send("b_ahead_1", b.at[pl.ds(half_b, half_b)], in_b(z, xh, half_b, sb), ahead)
    send("b_behind_0", b.at[pl.ds(0, half_b)], in_b(z, xh, 0, half_b), behind)
    send(("side", 0), own_a(0, 0, FIRST), in_a(0, y, xl, 0, FIRST), side)
    send_rest(0)
    send("b_sibling", b, in_b(z, xh, 0, sb), sibling)
    local = [pltpu.make_async_copy(own_a(h, 0, sa), in_a(h, y, xl, 0, sa), local_sem.at[h]) for h in range(HALVES)]
    local.append(pltpu.make_async_copy(b, in_b(z, xh, 0, sb), local_sem.at[2]))
    for copy in local:
        copy.start()

    def peer(offset, sign):
        dx, dy, dz, dc = offset
        xx = (x + 4 + sign * dx) % 4
        return device((y + 4 + sign * dy) % 4, xx % 2, (z + 4 + sign * dz) % 4, xx // 2, (core + dc) % 2)

    def b_source(s):
        return (s + j + COLS - i) % ROWS

    def multiply(h, yy, xx):
        s = yy * 2 + xx
        for part in range(2):
            source = b_source(s) + ROWS * part

            @pl.loop(0, width // 2 // 4)
            def _(quarter):
                for step in range(4):
                    k = quarter * 4 + step
                    first_a = s * sa + (part * width // 2 + k) * PER_K
                    left = a_panels[h, pl.ds(first_a, PER_K)].reshape(PER_K * rows, LANES)
                    at = s * per_panel + (part * width // 2 + k) * PER_K * PER_K
                    right = jnp.concatenate([b_panels[source * sb + k * PER_K + n] for n in range(PER_K)], axis=1)
                    out = jnp.dot(left, right, preferred_element_type=jnp.float32)
                    for m in range(PER_K):
                        for n in range(PER_K):
                            products[at + m * PER_K + n] = out[m * rows : (m + 1) * rows, n * LANES : (n + 1) * LANES]

    def multiply_others(h):
        multiply(h, y_last, xl)
        multiply(h, y_next, xl)
        arrived_a(h, "rest")
        multiply(h, y, xl_other)
        arrived_a(h, "last_side")
        multiply(h, y_last, xl_other)
        arrived_a(h, "next_side")
        multiply(h, y_next, xl_other)
        arrived_a(h, "side_last_up", "side_next_down", "far_side")
        multiply(h, y_far, xl_other)

    def add(group, r, total):
        product = products[index[group, r]]
        total = jnp.where(index[groups + group, r] > 0, product, total + product)
        sums[group * LANES + r] = total.astype(sums.dtype)
        return total

    def add_all():
        total = jnp.zeros((rows, LANES), jnp.float32)
        for group in range(groups):
            total = lax.fori_loop(0, LANES, functools.partial(add, group), total, unroll=8)

    def pack(h, t):
        for member in range(PAIR):
            at = PAIR * t + member
            block = sums[index[8 + at // LANES, at % LANES]]
            packed[h, at] = jnp.where(index[10 + at // LANES, at % LANES] > 0, block, jnp.zeros_like(block))

    mine = pl.ds(PAIR * me, PAIR)

    def send_blocks(h, some):
        for offset in some:
            other = peer(offset, 1 - 2 * core)
            t = other[0] * COLS + other[1]
            pack(h, t)
            pltpu.make_async_remote_copy(
                src_ref=packed.at[h, pl.ds(PAIR * t, PAIR)],
                dst_ref=got_blocks.at[h, mine],
                send_sem=block_send.at[h],
                recv_sem=block_recv.at[h],
                device_id=other,
                device_id_type=MESH,
            ).start()

    def keep_blocks(h):
        pack(h, me)
        copy = pltpu.make_async_copy(packed.at[h, mine], got_blocks.at[h, mine], local_sem.at[5 + h])
        copy.start()
        return copy

    arrived("b_ahead_0")
    pass_on("b_last_ahead", in_b(z_last, xh, 0, half_b), ahead)
    arrived("b_behind_1")
    pass_on("b_next_behind", in_b(z_next, xh, half_b, sb), behind)
    arrived("b_across_0")
    pass_on("b_across_ahead_0", in_b(z, xh_other, 0, half_b), ahead)
    pass_on("b_across_behind_0", in_b(z, xh_other, 0, half_b), behind)
    arrived("b_across_1")
    pass_on("b_across_behind_1", in_b(z, xh_other, half_b, sb), behind)
    pass_on("b_across_ahead_1", in_b(z, xh_other, half_b, sb), ahead)
    pass_on("b_across_sibling", in_b(z, xh_other, 0, sb), sibling)

    keep_col, owner_row, owner_col, slot_col = column(raw[2:3]), raw[3:4], column(raw[3:4]), column(raw[4:5])
    earlier = count((owner_col == owner_row) & (lane < sub), 1)
    place_col = jnp.where(owner_col >= 0, owner_col * PAIR + earlier, -1)
    slot_info[...] = SLOTS * (1 + PACK) + pick(
        owner_col == lane, (slot_col - SLOTS) * jnp.where(earlier == 0, 1, PACK)
    )

    for d in range(ROWS - 1):
        arrived(("row", d))
    for d in range(COLS - 1):
        arrived(("col", d))
    for mate in row_mates:
        pl.semaphore_signal(ready, inc=1, device_id=mate, device_id_type=MESH)

    def b_targets(s):
        return col_info[b_source(s)] + col_info[b_source(s) + ROWS]

    groups = ROWS // 2
    target_row = [
        row_info[2 * g] + row_info[2 * g + 1] + jnp.where(lane_row < per_panel, b_targets(2 * g), b_targets(2 * g + 1))
        for g in range(groups)
    ]
    target_col = [column(row) for row in target_row]
    rank, first = [], []
    for u in range(groups):
        before = jnp.zeros((LANES, LANES), jnp.int32)
        same = jnp.zeros((LANES, LANES), jnp.int32)
        for v in range(groups):
            lower = target_row[v] < target_col[u]
            equal = target_row[v] == target_col[u]
            if v == u:
                equal = equal & (lane < sub)
            if v <= u:
                before += (lower | equal).astype(jnp.int32)
                same += equal.astype(jnp.int32)
            else:
                before += lower.astype(jnp.int32)
        rank.append(jnp.sum(before, axis=1, keepdims=True))
        first.append((jnp.sum(same, axis=1, keepdims=True) == 0).astype(jnp.int32))
    for w in range(groups):
        here = [rank[u] == w * LANES + lane for u in range(groups)]
        table[w : w + 1] = sum(pick(here[u], u * LANES + sub) for u in range(groups))
        table[groups + w : groups + w + 1] = sum(pick(here[u], first[u]) for u in range(groups))
    for w in range(SLOTS // LANES):
        kept = pick(place_col == w * LANES + lane, keep_col + 1) - 1
        upto = sum(count(target_col[u] <= kept, 0) for u in range(groups))
        equal = sum(count(target_col[u] == kept, 0) for u in range(groups))
        table[8 + w : 9 + w] = jnp.maximum(upto - 1, 0)
        table[10 + w : 11 + w] = (equal > 0).astype(jnp.int32)
    to_scalars = pltpu.make_async_copy(table, index, local_sem.at[3])
    to_scalars.start()
    arrived("b_ahead_1", "b_behind_0")
    pass_on("b_last_sibling", in_b(z_last, xh, 0, sb), sibling)
    pass_on("b_next_sibling", in_b(z_next, xh, 0, sb), sibling)
    forward_near(0)
    forward_side(0)
    send_own(1)
    send_rest(1)
    pl.semaphore_wait(ready, ROWS - 1)

    @pl.loop(1, DEVICES)
    def _(o):
        pltpu.make_async_remote_copy(
            src_ref=slot_info,
            dst_ref=got_slots.at[me],
            send_sem=slot_send,
            recv_sem=slot_recv,
            device_id=peer((o // 2, o // 8, o // 32, o), 1),
            device_id_type=MESH,
        ).start()

    local_slots = pltpu.make_async_copy(slot_info, got_slots.at[me], local_sem.at[4])
    local_slots.start()

    arrived("b_last_ahead", "b_next_behind")
    pass_on("b_far_sibling", in_b(z_far, xh, 0, sb), sibling)
    arrived("b_across_ahead_0")
    pass_on("b_across_last_ahead", in_b(z_last, xh_other, 0, half_b), ahead)
    arrived("b_across_behind_1")
    pass_on("b_across_next_behind", in_b(z_next, xh_other, half_b, sb), behind)
    forward_far(0)
    arrived("b_across_ahead_1", "b_across_behind_0")
    pass_on("b_across_last_sibling", in_b(z_last, xh_other, 0, sb), sibling)
    pass_on("b_across_next_sibling", in_b(z_next, xh_other, 0, sb), sibling)
    forward_last(0)
    for copy in local:
        copy.wait()
    multiply(0, y, xl)
    arrived_a(0, "last_up")
    multiply(0, y_far, xl)
    arrived("b_across_last_ahead", "b_across_next_behind")
    pass_on("b_across_far_sibling", in_b(z_far, xh_other, 0, sb), sibling)
    forward_near(1)
    forward_side(1)
    arrived(
        "b_sibling", "b_last_sibling", "b_next_sibling", "b_across_sibling", "b_far_sibling",
        "b_across_last_sibling", "b_across_next_sibling", "b_across_far_sibling",
    )
    multiply_others(0)
    to_scalars.wait()
    add_all()
    every = offsets()
    send_blocks(0, every[:24])
    forward_far(1)
    send_blocks(0, every[24:48])
    forward_last(1)
    send_blocks(0, every[48:])
    kept = [keep_blocks(0)]
    multiply(1, y, xl)
    arrived_a(1, "last_up")
    multiply(1, y_far, xl)
    multiply_others(1)
    add_all()
    send_blocks(1, every)
    kept.append(keep_blocks(1))

    others = pl.ds(0, DEVICES - 1)
    every_slot = pltpu.make_async_remote_copy(
        src_ref=got_slots.at[others],
        dst_ref=got_slots.at[others],
        send_sem=slot_send,
        recv_sem=slot_recv,
        device_id=sibling,
        device_id_type=MESH,
    )
    every_slot.wait_recv()
    every_slot.wait_send()
    local_slots.wait()
    from_all = column_of(got_slots[...].reshape(DEVICES, LANES), me)
    goes = [from_all // PACK if member else from_all % PACK for member in range(PAIR)]
    places[...] = jnp.zeros(places.shape, jnp.int32)
    for w in range(SLOTS // LANES):
        source = sum(pick(goes[member] == w * LANES + lane, PAIR * sub + member - SLOTS) for member in range(PAIR))
        places[w : w + 1] = source + SLOTS
    for copy in copies.values():
        copy.wait_send()
    others = pl.ds(0, PAIR * (DEVICES - 1))
    for h in range(HALVES):
        every_block = pltpu.make_async_remote_copy(
            src_ref=packed.at[h, others],
            dst_ref=got_blocks.at[h, others],
            send_sem=block_send.at[h],
            recv_sem=block_recv.at[h],
            device_id=sibling,
            device_id_type=MESH,
        )
        every_block.wait_recv()
        every_block.wait_send()
        kept[h].wait()


def combine(a, b, a_rows, b_cols, keep, owner, slot):
    sa, sb = a.shape[0], b.shape[0]
    rows = LANES // HALVES
    product_count = ROWS * (sa // PER_K) * PER_K * PER_K
    messages = 2 * 13 + 24 + ROWS - 1 + COLS - 1
    anywhere = pl.BlockSpec(memory_space=pl.ANY)
    vmem = pl.BlockSpec(memory_space=pltpu.VMEM)
    return pl.pallas_call(
        functools.partial(combine_kernel, sa, sb),
        out_shape=(
            jax.ShapeDtypeStruct((HALVES, SLOTS, rows, LANES), a.dtype),
            jax.ShapeDtypeStruct((8, LANES), jnp.int32),
        ),
        in_specs=[anywhere] * 2 + [vmem] * 5,
        out_specs=[anywhere, vmem],
        scratch_shapes=[
            pltpu.VMEM((HALVES, ROWS * sa, rows, LANES), a.dtype),
            pltpu.VMEM((COLS * sb, LANES, LANES), a.dtype),
            pltpu.VMEM((product_count, rows, LANES), jnp.float32),
            pltpu.VMEM((product_count, rows, LANES), a.dtype),
            pltpu.VMEM((HALVES, SLOTS, rows, LANES), a.dtype),
            pltpu.VMEM((8, LANES), jnp.int32),
            pltpu.VMEM((ROWS, 1, LANES), jnp.int32),
            pltpu.VMEM((COLS, 1, LANES), jnp.int32),
            pltpu.VMEM((1, LANES), jnp.int32),
            pltpu.VMEM((DEVICES, 1, LANES), jnp.int32),
            pltpu.VMEM((16, LANES), jnp.int32),
            pltpu.SMEM((16, LANES), jnp.int32),
            pltpu.SemaphoreType.DMA((messages,)),
            pltpu.SemaphoreType.DMA((messages,)),
            pltpu.SemaphoreType.DMA((7,)),
            pltpu.SemaphoreType.REGULAR,
            pltpu.SemaphoreType.DMA((HALVES,)),
            pltpu.SemaphoreType.DMA((HALVES,)),
            pltpu.SemaphoreType.DMA,
            pltpu.SemaphoreType.DMA,
        ],
        compiler_params=pltpu.CompilerParams(
            collective_id=0, has_side_effects=True, vmem_limit_bytes=56 * 1024 * 1024
        ),
        name="combine",
    )(a, b, a_rows, b_cols, keep, owner, slot)


def place_kernel(places, blocks, owned, held, laid, load_sem, store_sem):
    parts = load_sem.shape[1]
    size = SLOTS // parts
    rows = blocks.shape[2]

    def load(h, part):
        at = pl.ds(part * size, size)
        return pltpu.make_async_copy(blocks.at[h, at], held.at[h, at], load_sem.at[h, part])

    def store(part):
        at = pl.ds(part * size, size)
        return pltpu.make_async_copy(laid.at[at], owned.at[at], store_sem.at[part])

    every = [(h, part) for h in range(HALVES) for part in range(parts)]
    for h, part in every:
        load(h, part).start()
    for h in range(HALVES):
        held[h, SLOTS] = jnp.zeros((rows, LANES), held.dtype)
    for h, part in every:
        load(h, part).wait()
    for part in range(2 * parts):

        @pl.loop(0, size // 2, unroll=4)
        def _(n):
            slot = part * (size // 2) + n
            source = places[slot // LANES, slot % LANES]
            for h in range(HALVES):
                laid[slot, h * rows : (h + 1) * rows] = held[h, source]

        if part % 2:
            store(part // 2).start()
    for part in range(parts):
        store(part).wait()


def place_blocks(places, blocks):
    rows = blocks.shape[2]
    parts = 8
    return pl.pallas_call(
        place_kernel,
        out_shape=jax.ShapeDtypeStruct((SLOTS, LANES, LANES), blocks.dtype),
        in_specs=[pl.BlockSpec(memory_space=pltpu.SMEM), pl.BlockSpec(memory_space=pl.ANY)],
        out_specs=pl.BlockSpec(memory_space=pl.ANY),
        scratch_shapes=[
            pltpu.VMEM((HALVES, SLOTS + 1, rows, LANES), blocks.dtype),
            pltpu.VMEM((SLOTS, LANES, LANES), blocks.dtype),
            pltpu.SemaphoreType.DMA((HALVES, parts)),
            pltpu.SemaphoreType.DMA((parts,)),
        ],
        compiler_params=pltpu.CompilerParams(vmem_limit_bytes=56 * 1024 * 1024),
        name="place",
    )(places, blocks)


def body(a_blocks, a_rows, b_blocks, b_cols, c_keep, c_owner, c_slot):
    got_blocks, places = combine(a_blocks[0], b_blocks[0], a_rows, b_cols, c_keep[0], c_owner[0], c_slot[0])
    return place_blocks(places, got_blocks)[None]


def solution(mesh):
    return jax.shard_map(
        body,
        mesh=mesh,
        in_specs=(
            P("col", "row", None, None),
            P("col", "row"),
            P("row", "col", None, None),
            P("row", "col"),
            P("row", "col", None),
            P("row", "col", None),
            P("row", "col", None),
        ),
        out_specs=P("row", "col", None, None),
        check_vma=False,
    )
```

```python
import functools
import itertools
import random

import jax
import jax.numpy as jnp
from jax import lax
from jax.experimental import pallas as pl
from jax.experimental.pallas import tpu as pltpu
from jax.sharding import PartitionSpec as P

MESH = pl.DeviceIdType.MESH
ROWS, COLS = 8, 16
DEVICES = ROWS * COLS
PER_K = 2
PAIR = 2
LANES = 128
FIRST = 22
SLOTS = PAIR * DEVICES
PACK = 512
HALVES = 2


def coordinates():
    i, j = lax.axis_index("row"), lax.axis_index("col")
    return i // 2, i % 2, j // 4, (j // 2) % 2, j % 2


def device(y, xl, z, xh, core):
    return (y * 2 + xl, (z * 2 + xh) * 2 + core)


def offsets():
    every = [o for o in itertools.product(range(4), range(4), range(4), range(2)) if any(o)]
    random.Random(3).shuffle(every)
    return every


def iota(axis):
    return lax.broadcasted_iota(jnp.int32, (LANES, LANES), axis)


def column(row):
    return jnp.sum(jnp.where(iota(0) == iota(1), row, 0), axis=1, keepdims=True)


def column_of(values, at):
    return jnp.sum(jnp.where(iota(1) == at, values, 0), axis=1, keepdims=True)


def count(mask, axis):
    return jnp.sum(mask.astype(jnp.int32), axis=axis, keepdims=True)


def pick(mask, values):
    return jnp.sum(jnp.where(mask, values, 0), axis=0, keepdims=True)


def combine_kernel(
    sa, sb, a, b, a_rows, b_cols, keep, owner, slot, got_blocks, places,
    a_panels, b_panels, products, sums, packed, raw, row_info, col_info, slot_info, got_slots, table, index,
    send_sem, recv_sem, local_sem, ready, block_send, block_recv, slot_send, slot_recv,
):
    y, xl, z, xh, core = coordinates()
    x = xh * 2 + xl
    i, j = y * 2 + xl, (z * 2 + xh) * 2 + core
    me = i * COLS + j
    width = sa // PER_K
    per_panel = width * PER_K * PER_K
    rows = LANES // HALVES
    y_next, y_last, y_far = (y + 1) % 4, (y + 3) % 4, (y + 2) % 4
    z_next, z_last, z_far = (z + 1) % 4, (z + 3) % 4, (z + 2) % 4
    xl_other, xh_other = 1 - xl, 1 - xh
    up, down = device(y_next, xl, z, xh, core), device(y_last, xl, z, xh, core)
    ahead, behind = device(y, xl, z_next, xh, core), device(y, xl, z_last, xh, core)
    side, across = device(y, xl_other, z, xh, core), device(y, xl, z, xh_other, core)
    sibling = device(y, xl, z, xh, 1 - core)
    row_mates = [((i + d) % ROWS, j) for d in range(1, ROWS)]
    col_mates = [(i, (j + d) % COLS) for d in range(1, COLS)]

    barrier = pltpu.get_barrier_semaphore()
    for mate in row_mates + col_mates:
        pl.semaphore_signal(barrier, inc=1, device_id=mate, device_id_type=MESH)
    sub, lane = iota(0), iota(1)
    lane_row = lane[0:1]
    raw[...] = jnp.full(raw.shape, -1, jnp.int32)
    raw[0:1, 0:sa] = a_rows[...]
    raw[1:2, 0:sb] = b_cols[...]
    raw[2:3, 0 : keep.shape[1]] = keep[...]
    raw[3:4, 0 : owner.shape[1]] = owner[...]
    raw[4:5, 0 : slot.shape[1]] = slot[...]
    within = lane % per_panel
    a_lanes = pick(sub == (within // 4) * 2 + (within // 2) % 2, column(raw[0:1]) * width)
    row_info[i] = jnp.where(lane_row // per_panel == i % 2, a_lanes, 0)
    of_half = within - (per_panel // 2) * (j // ROWS)
    b_lanes = pick((sub == (of_half // 4) * 2 + of_half % 2) & (of_half >= 0) & (of_half < per_panel // 2), column(raw[1:2]))
    col_info[j] = b_lanes
    pl.semaphore_wait(barrier, ROWS + COLS - 2)

    def in_a(h, yy, xx, lo, hi):
        return a_panels.at[h, pl.ds((yy * 2 + xx) * sa + lo, hi - lo)]

    def own_a(h, lo, hi):
        return a.at[pl.ds(lo, hi - lo), pl.ds(h * rows, rows)]

    def in_b(zz, hh, lo, hi):
        return b_panels.at[pl.ds(((zz * 2 + hh) * 2 + core) * sb + lo, hi - lo)]

    copies = {}

    def send(name, src, dst, to):
        k = len(copies)
        copies[name] = pltpu.make_async_remote_copy(
            src_ref=src,
            dst_ref=dst,
            send_sem=send_sem.at[k],
            recv_sem=recv_sem.at[k],
            device_id=to,
            device_id_type=MESH,
        )
        copies[name].start()

    def pass_on(name, block, to):
        send(name, block, block, to)

    def arrived(*names):
        for name in names:
            copies[name].wait_recv()

    def arrived_a(h, *names):
        arrived(*((name, h) for name in names))

    half_a, half_b, half_first = sa // 2, sb // 2, FIRST // 2

    def send_own(h):
        send(("up", h), own_a(h, 0, sa), in_a(h, y, xl, 0, sa), up)
        send(("down", h), own_a(h, 0, sa), in_a(h, y, xl, 0, sa), down)
        send(("side", h), own_a(h, 0, FIRST), in_a(h, y, xl, 0, FIRST), side)

    def send_rest(h):
        send(("rest", h), own_a(h, FIRST, sa), in_a(h, y, xl, FIRST, sa), side)

    def forward_near(h):
        arrived_a(h, "up")
        pass_on(("last_up", h), in_a(h, y_last, xl, 0, half_a), up)
        pass_on(("last_side", h), in_a(h, y_last, xl, FIRST, sa), side)
        arrived_a(h, "down")
        pass_on(("next_down", h), in_a(h, y_next, xl, half_a, sa), down)
        pass_on(("next_side", h), in_a(h, y_next, xl, FIRST, sa), side)

    def forward_side(h):
        arrived_a(h, "side")
        pass_on(("side_up", h), in_a(h, y, xl_other, 0, FIRST), up)
        pass_on(("side_down", h), in_a(h, y, xl_other, 0, FIRST), down)

    def forward_far(h):
        arrived_a(h, "next_down")
        pass_on(("far_side", h), in_a(h, y_far, xl, FIRST, sa), side)

    def forward_last(h):
        arrived_a(h, "side_up")
        pass_on(("side_last_up", h), in_a(h, y_last, xl_other, 0, half_first), up)
        arrived_a(h, "side_down")
        pass_on(("side_next_down", h), in_a(h, y_next, xl_other, half_first, FIRST), down)

    for d, mate in enumerate(row_mates):
        pass_on(("row", d), row_info.at[i], mate)
    for d, mate in enumerate(col_mates):
        pass_on(("col", d), col_info.at[j], mate)
    send("b_across_0", b.at[pl.ds(0, half_b)], in_b(z, xh, 0, half_b), across)
    send("b_across_1", b.at[pl.ds(half_b, half_b)], in_b(z, xh, half_b, sb), across)
    send("b_ahead_0", b.at[pl.ds(0, half_b)], in_b(z, xh, 0, half_b), ahead)
    send("b_behind_1", b.at[pl.ds(half_b, half_b)], in_b(z, xh, half_b, sb), behind)
    send(("up", 0), own_a(0, 0, sa), in_a(0, y, xl, 0, sa), up)
    send(("down", 0), own_a(0, 0, sa), in_a(0, y, xl, 0, sa), down)
    send("b_ahead_1", b.at[pl.ds(half_b, half_b)], in_b(z, xh, half_b, sb), ahead)
    send("b_behind_0", b.at[pl.ds(0, half_b)], in_b(z, xh, 0, half_b), behind)
    send(("side", 0), own_a(0, 0, FIRST), in_a(0, y, xl, 0, FIRST), side)
    send_rest(0)
    send("b_sibling", b, in_b(z, xh, 0, sb), sibling)
    local = [pltpu.make_async_copy(own_a(h, 0, sa), in_a(h, y, xl, 0, sa), local_sem.at[h]) for h in range(HALVES)]
    local.append(pltpu.make_async_copy(b, in_b(z, xh, 0, sb), local_sem.at[2]))
    for copy in local:
        copy.start()

    def peer(offset, sign):
        dx, dy, dz, dc = offset
        xx = (x + 4 + sign * dx) % 4
        return device((y + 4 + sign * dy) % 4, xx % 2, (z + 4 + sign * dz) % 4, xx // 2, (core + dc) % 2)

    def b_source(s):
        return (s + j + COLS - i) % ROWS

    def multiply(h, yy, xx):
        s = yy * 2 + xx
        for part in range(2):
            source = b_source(s) + ROWS * part

            @pl.loop(0, width // 2 // 4)
            def _(quarter):
                for step in range(4):
                    k = quarter * 4 + step
                    first_a = s * sa + (part * width // 2 + k) * PER_K
                    left = a_panels[h, pl.ds(first_a, PER_K)].reshape(PER_K * rows, LANES)
                    at = s * per_panel + (part * width // 2 + k) * PER_K * PER_K
                    right = jnp.concatenate([b_panels[source * sb + k * PER_K + n] for n in range(PER_K)], axis=1)
                    out = jnp.dot(left, right, preferred_element_type=jnp.float32)
                    for m in range(PER_K):
                        for n in range(PER_K):
                            products[at + m * PER_K + n] = out[m * rows : (m + 1) * rows, n * LANES : (n + 1) * LANES]

    def multiply_others(h):
        multiply(h, y_last, xl)
        multiply(h, y_next, xl)
        arrived_a(h, "rest")
        multiply(h, y, xl_other)
        arrived_a(h, "last_side")
        multiply(h, y_last, xl_other)
        arrived_a(h, "next_side")
        multiply(h, y_next, xl_other)
        arrived_a(h, "side_last_up", "side_next_down", "far_side")
        multiply(h, y_far, xl_other)

    def add(group, r, total):
        product = products[index[group, r]]
        total = jnp.where(index[groups + group, r] > 0, product, total + product)
        sums[group * LANES + r] = total.astype(sums.dtype)
        return total

    def add_all():
        total = jnp.zeros((rows, LANES), jnp.float32)
        for group in range(groups):
            total = lax.fori_loop(0, LANES, functools.partial(add, group), total, unroll=8)

    def pack(h, t):
        for member in range(PAIR):
            at = PAIR * t + member
            block = sums[index[8 + at // LANES, at % LANES]]
            packed[h, at] = jnp.where(index[10 + at // LANES, at % LANES] > 0, block, jnp.zeros_like(block))

    mine = pl.ds(PAIR * me, PAIR)

    def send_blocks(h, some):
        for offset in some:
            other = peer(offset, 1 - 2 * core)
            t = other[0] * COLS + other[1]
            pack(h, t)
            pltpu.make_async_remote_copy(
                src_ref=packed.at[h, pl.ds(PAIR * t, PAIR)],
                dst_ref=got_blocks.at[h, mine],
                send_sem=block_send.at[h],
                recv_sem=block_recv.at[h],
                device_id=other,
                device_id_type=MESH,
            ).start()

    def keep_blocks(h):
        pack(h, me)
        copy = pltpu.make_async_copy(packed.at[h, mine], got_blocks.at[h, mine], local_sem.at[5 + h])
        copy.start()
        return copy

    arrived("b_ahead_0")
    pass_on("b_last_ahead", in_b(z_last, xh, 0, half_b), ahead)
    arrived("b_behind_1")
    pass_on("b_next_behind", in_b(z_next, xh, half_b, sb), behind)
    arrived("b_across_0")
    pass_on("b_across_ahead_0", in_b(z, xh_other, 0, half_b), ahead)
    pass_on("b_across_behind_0", in_b(z, xh_other, 0, half_b), behind)
    arrived("b_across_1")
    pass_on("b_across_behind_1", in_b(z, xh_other, half_b, sb), behind)
    pass_on("b_across_ahead_1", in_b(z, xh_other, half_b, sb), ahead)
    pass_on("b_across_sibling", in_b(z, xh_other, 0, sb), sibling)

    keep_col, owner_row, owner_col, slot_col = column(raw[2:3]), raw[3:4], column(raw[3:4]), column(raw[4:5])
    earlier = count((owner_col == owner_row) & (lane < sub), 1)
    place_col = jnp.where(owner_col >= 0, owner_col * PAIR + earlier, -1)
    slot_info[...] = SLOTS * (1 + PACK) + pick(
        owner_col == lane, (slot_col - SLOTS) * jnp.where(earlier == 0, 1, PACK)
    )

    for d in range(ROWS - 1):
        arrived(("row", d))
    for d in range(COLS - 1):
        arrived(("col", d))
    for mate in row_mates:
        pl.semaphore_signal(ready, inc=1, device_id=mate, device_id_type=MESH)

    def b_targets(s):
        return col_info[b_source(s)] + col_info[b_source(s) + ROWS]

    groups = ROWS // 2
    target_row = [
        row_info[2 * g] + row_info[2 * g + 1] + jnp.where(lane_row < per_panel, b_targets(2 * g), b_targets(2 * g + 1))
        for g in range(groups)
    ]
    target_col = [column(row) for row in target_row]
    rank, first = [], []
    for u in range(groups):
        before = jnp.zeros((LANES, LANES), jnp.int32)
        same = jnp.zeros((LANES, LANES), jnp.int32)
        for v in range(groups):
            lower = target_row[v] < target_col[u]
            equal = target_row[v] == target_col[u]
            if v == u:
                equal = equal & (lane < sub)
            if v <= u:
                before += (lower | equal).astype(jnp.int32)
                same += equal.astype(jnp.int32)
            else:
                before += lower.astype(jnp.int32)
        rank.append(jnp.sum(before, axis=1, keepdims=True))
        first.append((jnp.sum(same, axis=1, keepdims=True) == 0).astype(jnp.int32))
    for w in range(groups):
        here = [rank[u] == w * LANES + lane for u in range(groups)]
        table[w : w + 1] = sum(pick(here[u], u * LANES + sub) for u in range(groups))
        table[groups + w : groups + w + 1] = sum(pick(here[u], first[u]) for u in range(groups))
    for w in range(SLOTS // LANES):
        kept = pick(place_col == w * LANES + lane, keep_col + 1) - 1
        upto = sum(count(target_col[u] <= kept, 0) for u in range(groups))
        equal = sum(count(target_col[u] == kept, 0) for u in range(groups))
        table[8 + w : 9 + w] = jnp.maximum(upto - 1, 0)
        table[10 + w : 11 + w] = (equal > 0).astype(jnp.int32)
    to_scalars = pltpu.make_async_copy(table, index, local_sem.at[3])
    to_scalars.start()
    arrived("b_ahead_1", "b_behind_0")
    pass_on("b_last_sibling", in_b(z_last, xh, 0, sb), sibling)
    pass_on("b_next_sibling", in_b(z_next, xh, 0, sb), sibling)
    forward_near(0)
    send_own(1)
    forward_side(0)
    send_rest(1)
    pl.semaphore_wait(ready, ROWS - 1)

    @pl.loop(1, DEVICES)
    def _(o):
        pltpu.make_async_remote_copy(
            src_ref=slot_info,
            dst_ref=got_slots.at[me],
            send_sem=slot_send,
            recv_sem=slot_recv,
            device_id=peer((o // 2, o // 8, o // 32, o), 1),
            device_id_type=MESH,
        ).start()

    local_slots = pltpu.make_async_copy(slot_info, got_slots.at[me], local_sem.at[4])
    local_slots.start()

    arrived("b_last_ahead", "b_next_behind")
    pass_on("b_far_sibling", in_b(z_far, xh, 0, sb), sibling)
    arrived("b_across_ahead_0")
    pass_on("b_across_last_ahead", in_b(z_last, xh_other, 0, half_b), ahead)
    arrived("b_across_behind_1")
    pass_on("b_across_next_behind", in_b(z_next, xh_other, half_b, sb), behind)
    forward_far(0)
    arrived("b_across_ahead_1", "b_across_behind_0")
    pass_on("b_across_last_sibling", in_b(z_last, xh_other, 0, sb), sibling)
    pass_on("b_across_next_sibling", in_b(z_next, xh_other, 0, sb), sibling)
    forward_near(1)
    forward_last(0)
    for copy in local:
        copy.wait()
    multiply(0, y, xl)
    arrived_a(0, "last_up")
    multiply(0, y_far, xl)
    arrived("b_across_last_ahead", "b_across_next_behind")
    pass_on("b_across_far_sibling", in_b(z_far, xh_other, 0, sb), sibling)
    forward_side(1)
    arrived(
        "b_sibling", "b_last_sibling", "b_next_sibling", "b_across_sibling", "b_far_sibling",
        "b_across_last_sibling", "b_across_next_sibling", "b_across_far_sibling",
    )
    multiply_others(0)
    to_scalars.wait()
    add_all()
    every = offsets()
    send_blocks(0, every[:24])
    forward_far(1)
    send_blocks(0, every[24:48])
    forward_last(1)
    send_blocks(0, every[48:])
    kept = [keep_blocks(0)]
    multiply(1, y, xl)
    arrived_a(1, "last_up")
    multiply(1, y_far, xl)
    multiply_others(1)
    add_all()
    send_blocks(1, every)
    kept.append(keep_blocks(1))

    others = pl.ds(0, DEVICES - 1)
    every_slot = pltpu.make_async_remote_copy(
        src_ref=got_slots.at[others],
        dst_ref=got_slots.at[others],
        send_sem=slot_send,
        recv_sem=slot_recv,
        device_id=sibling,
        device_id_type=MESH,
    )
    every_slot.wait_recv()
    every_slot.wait_send()
    local_slots.wait()
    from_all = column_of(got_slots[...].reshape(DEVICES, LANES), me)
    goes = [from_all // PACK if member else from_all % PACK for member in range(PAIR)]
    places[...] = jnp.zeros(places.shape, jnp.int32)
    for w in range(SLOTS // LANES):
        source = sum(pick(goes[member] == w * LANES + lane, PAIR * sub + member - SLOTS) for member in range(PAIR))
        places[w : w + 1] = source + SLOTS
    for copy in copies.values():
        copy.wait_send()
    others = pl.ds(0, PAIR * (DEVICES - 1))
    for h in range(HALVES):
        every_block = pltpu.make_async_remote_copy(
            src_ref=packed.at[h, others],
            dst_ref=got_blocks.at[h, others],
            send_sem=block_send.at[h],
            recv_sem=block_recv.at[h],
            device_id=sibling,
            device_id_type=MESH,
        )
        every_block.wait_recv()
        every_block.wait_send()
        kept[h].wait()


def combine(a, b, a_rows, b_cols, keep, owner, slot):
    sa, sb = a.shape[0], b.shape[0]
    rows = LANES // HALVES
    product_count = ROWS * (sa // PER_K) * PER_K * PER_K
    messages = 2 * 13 + 24 + ROWS - 1 + COLS - 1
    anywhere = pl.BlockSpec(memory_space=pl.ANY)
    vmem = pl.BlockSpec(memory_space=pltpu.VMEM)
    return pl.pallas_call(
        functools.partial(combine_kernel, sa, sb),
        out_shape=(
            jax.ShapeDtypeStruct((HALVES, SLOTS, rows, LANES), a.dtype),
            jax.ShapeDtypeStruct((8, LANES), jnp.int32),
        ),
        in_specs=[anywhere] * 2 + [vmem] * 5,
        out_specs=[anywhere, vmem],
        scratch_shapes=[
            pltpu.VMEM((HALVES, ROWS * sa, rows, LANES), a.dtype),
            pltpu.VMEM((COLS * sb, LANES, LANES), a.dtype),
            pltpu.VMEM((product_count, rows, LANES), jnp.float32),
            pltpu.VMEM((product_count, rows, LANES), a.dtype),
            pltpu.VMEM((HALVES, SLOTS, rows, LANES), a.dtype),
            pltpu.VMEM((8, LANES), jnp.int32),
            pltpu.VMEM((ROWS, 1, LANES), jnp.int32),
            pltpu.VMEM((COLS, 1, LANES), jnp.int32),
            pltpu.VMEM((1, LANES), jnp.int32),
            pltpu.VMEM((DEVICES, 1, LANES), jnp.int32),
            pltpu.VMEM((16, LANES), jnp.int32),
            pltpu.SMEM((16, LANES), jnp.int32),
            pltpu.SemaphoreType.DMA((messages,)),
            pltpu.SemaphoreType.DMA((messages,)),
            pltpu.SemaphoreType.DMA((7,)),
            pltpu.SemaphoreType.REGULAR,
            pltpu.SemaphoreType.DMA((HALVES,)),
            pltpu.SemaphoreType.DMA((HALVES,)),
            pltpu.SemaphoreType.DMA,
            pltpu.SemaphoreType.DMA,
        ],
        compiler_params=pltpu.CompilerParams(
            collective_id=0, has_side_effects=True, vmem_limit_bytes=56 * 1024 * 1024
        ),
        name="combine",
    )(a, b, a_rows, b_cols, keep, owner, slot)


def place_kernel(places, blocks, owned, held, laid, load_sem, store_sem):
    parts = load_sem.shape[1]
    size = SLOTS // parts
    rows = blocks.shape[2]

    def load(h, part):
        at = pl.ds(part * size, size)
        return pltpu.make_async_copy(blocks.at[h, at], held.at[h, at], load_sem.at[h, part])

    def store(part):
        at = pl.ds(part * size, size)
        return pltpu.make_async_copy(laid.at[at], owned.at[at], store_sem.at[part])

    every = [(h, part) for h in range(HALVES) for part in range(parts)]
    for h, part in every:
        load(h, part).start()
    for h in range(HALVES):
        held[h, SLOTS] = jnp.zeros((rows, LANES), held.dtype)
    for h, part in every:
        load(h, part).wait()
    for part in range(2 * parts):

        @pl.loop(0, size // 2, unroll=4)
        def _(n):
            slot = part * (size // 2) + n
            source = places[slot // LANES, slot % LANES]
            for h in range(HALVES):
                laid[slot, h * rows : (h + 1) * rows] = held[h, source]

        if part % 2:
            store(part // 2).start()
    for part in range(parts):
        store(part).wait()


def place_blocks(places, blocks):
    rows = blocks.shape[2]
    parts = 8
    return pl.pallas_call(
        place_kernel,
        out_shape=jax.ShapeDtypeStruct((SLOTS, LANES, LANES), blocks.dtype),
        in_specs=[pl.BlockSpec(memory_space=pltpu.SMEM), pl.BlockSpec(memory_space=pl.ANY)],
        out_specs=pl.BlockSpec(memory_space=pl.ANY),
        scratch_shapes=[
            pltpu.VMEM((HALVES, SLOTS + 1, rows, LANES), blocks.dtype),
            pltpu.VMEM((SLOTS, LANES, LANES), blocks.dtype),
            pltpu.SemaphoreType.DMA((HALVES, parts)),
            pltpu.SemaphoreType.DMA((parts,)),
        ],
        compiler_params=pltpu.CompilerParams(vmem_limit_bytes=56 * 1024 * 1024),
        name="place",
    )(places, blocks)


def body(a_blocks, a_rows, b_blocks, b_cols, c_keep, c_owner, c_slot):
    got_blocks, places = combine(a_blocks[0], b_blocks[0], a_rows, b_cols, c_keep[0], c_owner[0], c_slot[0])
    return place_blocks(places, got_blocks)[None]


def solution(mesh):
    return jax.shard_map(
        body,
        mesh=mesh,
        in_specs=(
            P("col", "row", None, None),
            P("col", "row"),
            P("row", "col", None, None),
            P("row", "col"),
            P("row", "col", None),
            P("row", "col", None),
            P("row", "col", None),
        ),
        out_specs=P("row", "col", None, None),
        check_vma=False,
    )
```
